32 devices in a mesh: layer: 2 (over y), expert: 8 (over z, x), row: 2 (over core).
Axes of the slice: x: 2, y: 2, z: 4, core: 2. Of those that a mesh axis runs over, the one named last changes fastest.
Arguments:
- weights: bfloat16 [16, 1024, 3584], P(('layer', 'expert'), None, 'row'), parts along dimension 0, may hold values from -6 to 6
- factors: float32 [16, 1024, 128], P(('layer', 'expert'), 'row'), parts along dimension 0, may hold values from -6 to 6
- mixing: float32 [16, 64], P(('layer', 'expert')), parts along dimension 0, may hold values from -6 to 6
- shared_bases: float32 [7168, 64, 128], P(('layer', 'row', 'expert')), parts along dimension 0, may hold values from -6 to 6
Outputs:
- factors_new: float32 [16, 1024, 128], P(('layer', 'expert'), 'row'), parts along dimension 0
- bases_new: float32 [7168, 64, 128], P(('layer', 'row', 'expert')), parts along dimension 0
- mixing_new: float32 [16, 64], P(('layer', 'expert')), parts along dimension 0
The draws below stay inside these ranges and needn't reach their ends.
There are 2 independent parts, one for each index of `layer`. The reference program is written for one: setup_inputs(seed, part) draws one part's arguments, and reference() takes and returns one part's arrays. A program takes and returns all parts, laid end to end along the dimension named above; each array names one. Nothing has to cross between parts.
All inputs are finite; a program needn't handle non-finite values.
Results may differ from the reference program's by a relative error of at most 0.0014.
Values may be sent and summed in bfloat16 or wider, within the bound.
No kernel may reach another device: no remote copies, remote signals or barrier semaphores. Data moves between devices by JAX's collectives and lax.ppermute only.
A program may use at most 128 MiB of HBM per device.

```python
import math
import jax
import jax.numpy as jnp
from jax import lax

H = 1024
D = 3584
NB = 64
RANK = 128
ITERS = 2
EXPERTS = 8


def level_of(rng, extent, cuts, smallest, top_value):
    gain, own = 1.0, jax.random.fold_in(rng, 6)
    for position, blocks in cuts:
        steps = jnp.exp(jax.random.uniform(jax.random.fold_in(own, position), (blocks,), jnp.float32, smallest / len(cuts), top_value / len(cuts)))
        gain = gain * jnp.repeat(steps, extent[position] // blocks).reshape([-1 if axis == position else 1 for axis in range(len(extent))])
    return gain


def noise(stream_key, dims, deviation, limit, split=(), kind=jnp.bfloat16):
    array = deviation * jax.random.normal(stream_key, dims, jnp.float32)
    if split:
        array = array * level_of(stream_key, dims, split, -0.22, 0.18)
    return jnp.clip(array, -limit, limit).astype(kind)


def setup_inputs(seed: int = 0, part: int = 0) -> dict:
    key_of = jax.random.split(jax.random.key(seed), 5)
    part_keys = jax.random.split(jax.random.fold_in(key_of[4], part), 5)
    weights = noise(part_keys[0], (EXPERTS, H, D), 1.0, 6.0, ((0, 8), (2, 2)))
    factors = noise(part_keys[1], (EXPERTS, H, RANK), 1.0, 6.0, ((0, 8), (1, 2)), jnp.float32)
    mixing = noise(part_keys[2], (EXPERTS, NB), 1.0, 6.0, ((0, 8),), jnp.float32)
    shared_bases = noise(part_keys[3], (D, NB, RANK), 1.0, 6.0, ((0, 16),), jnp.float32)
    return {"weights": weights, "factors": factors, "mixing": mixing, "shared_bases": shared_bases}


BETA_ONE = 0.9
BETA_TWO = 0.999
RATE = 0.3
EPSILON_FACTORS = 8.0
EPSILON_BASES = 6.0
EPSILON_MIXING = 300.0

def adam_update(values, moment_one, moment_two, gradient, iteration, epsilon):
    moment_one = BETA_ONE * moment_one + (1.0 - BETA_ONE) * gradient
    moment_two = BETA_TWO * moment_two + (1.0 - BETA_TWO) * gradient * gradient
    correct_one = 1.0 - BETA_ONE ** iteration
    correct_two = 1.0 - BETA_TWO ** iteration
    values = values - RATE * (moment_one / correct_one) / (jnp.sqrt(moment_two / correct_two) + epsilon)
    return (values, moment_one, moment_two)

def per_expert(members):
    target, factor_low, panels = members
    residual = jnp.dot(factor_low, panels.T, preferred_element_type=jnp.float32) - target.astype(jnp.float32)
    residual_low = residual.astype(jnp.bfloat16)
    grad_factor = jnp.dot(residual_low, panels, preferred_element_type=jnp.float32)
    grad_panel = jnp.dot(residual_low.T, factor_low, preferred_element_type=jnp.float32)
    return (grad_factor, grad_panel)

def reference(weights, factors, mixing, shared_bases):
    mix_scale = 1.0 / math.sqrt(NB * RANK)
    factor_one = jnp.zeros(factors.shape, jnp.float32)
    factor_two = jnp.zeros(factors.shape, jnp.float32)
    bases_one = jnp.zeros(shared_bases.shape, jnp.float32)
    bases_two = jnp.zeros(shared_bases.shape, jnp.float32)
    mixing_one = jnp.zeros(mixing.shape, jnp.float32)
    mixing_two = jnp.zeros(mixing.shape, jnp.float32)
    for iteration in range(1, ITERS + 1):
        mixed = (mix_scale * jnp.einsum('ej,djr->edr', mixing, shared_bases, precision=lax.Precision.HIGHEST)).astype(jnp.bfloat16)
        factors_low = factors.astype(jnp.bfloat16)
        grad_factors, grad_panels = lax.map(per_expert, (weights, factors_low, mixed))
        grad_bases = mix_scale * jnp.einsum('ej,edr->djr', mixing, grad_panels, precision=lax.Precision.HIGHEST)
        grad_mixing = mix_scale * jnp.einsum('djr,edr->ej', shared_bases, grad_panels, precision=lax.Precision.HIGHEST)
        factors, factor_one, factor_two = adam_update(factors, factor_one, factor_two, grad_factors, iteration, EPSILON_FACTORS)
        shared_bases, bases_one, bases_two = adam_update(shared_bases, bases_one, bases_two, grad_bases, iteration, EPSILON_BASES)
        mixing, mixing_one, mixing_two = adam_update(mixing, mixing_one, mixing_two, grad_mixing, iteration, EPSILON_MIXING)
    return (factors, shared_bases, mixing)
```

```python
import functools
import math

import jax
import jax.numpy as jnp
from jax import lax
from jax.experimental import pallas as pl
from jax.experimental.pallas import tpu as pltpu
from jax.sharding import PartitionSpec as P

ITERS = 2


BETA_ONE = 0.9
BETA_TWO = 0.999
RATE = 0.3
EPSILON_FACTORS = 8.0
EPSILON_BASES = 6.0
EPSILON_MIXING = 300.0

FIRST_OLD = BETA_ONE * (1.0 - BETA_ONE) / (1.0 - BETA_ONE**2)
FIRST_NEW = (1.0 - BETA_ONE) / (1.0 - BETA_ONE**2)
SECOND_OLD = BETA_TWO * (1.0 - BETA_TWO) / (1.0 - BETA_TWO**2)
SECOND_NEW = (1.0 - BETA_TWO) / (1.0 - BETA_TWO**2)

GROUP = 16
CHUNK = 32
MEGABYTE = 1 << 20


def adam_update(values, moment_one, moment_two, gradient, iteration, epsilon):
    moment_one = BETA_ONE * moment_one + (1.0 - BETA_ONE) * gradient
    moment_two = BETA_TWO * moment_two + (1.0 - BETA_TWO) * gradient * gradient
    correct_one = 1.0 - BETA_ONE**iteration
    correct_two = 1.0 - BETA_TWO**iteration
    values = values - RATE * (moment_one / correct_one) / (
        jnp.sqrt(moment_two / correct_two) + epsilon
    )
    return (values, moment_one, moment_two)


def first_step(values, gradient, epsilon):
    return values - RATE * gradient / (jnp.abs(gradient) + epsilon)


def second_step(values, old, new, epsilon):
    values = first_step(values, old, epsilon)
    top = FIRST_OLD * old + FIRST_NEW * new
    root = jnp.sqrt(SECOND_OLD * (old * old) + SECOND_NEW * (new * new))
    return values - RATE * top / (root + epsilon)


def halves(array):
    high = array.astype(jnp.bfloat16)
    low = (array - high.astype(jnp.float32)).astype(jnp.bfloat16)
    return (high, low)


def dot(left, right, contract=((1,), (0,))):
    return lax.dot_general(left, right, (contract, ((), ())), preferred_element_type=jnp.float32)


def spread_rows(mixing, scale):
    experts, bases = mixing.shape
    rows, columns = experts * GROUP, GROUP * bases
    pick = (
        lax.broadcasted_iota(jnp.int32, (rows, experts), 0) // GROUP
        == lax.broadcasted_iota(jnp.int32, (rows, experts), 1)
    ).astype(jnp.bfloat16)
    tile = (
        lax.broadcasted_iota(jnp.int32, (bases, columns), 0)
        == lax.broadcasted_iota(jnp.int32, (bases, columns), 1) % bases
    ).astype(jnp.bfloat16)
    keep = (
        lax.broadcasted_iota(jnp.int32, (rows, columns), 0) % GROUP
        == lax.broadcasted_iota(jnp.int32, (rows, columns), 1) // bases
    )
    parts = []
    for half in halves(scale * mixing):
        wide = dot(half, tile).astype(jnp.bfloat16)
        parts.append(jnp.where(keep, dot(pick, wide), 0.0).astype(jnp.bfloat16))
    return jnp.concatenate(parts, axis=0)


def spread_columns(mixing, scale):
    experts, bases = mixing.shape
    rows, columns = GROUP * bases, experts * GROUP
    pick = (
        lax.broadcasted_iota(jnp.int32, (experts, columns), 0)
        == lax.broadcasted_iota(jnp.int32, (experts, columns), 1) // GROUP
    ).astype(jnp.bfloat16)
    tile = (
        lax.broadcasted_iota(jnp.int32, (rows, bases), 0) % bases
        == lax.broadcasted_iota(jnp.int32, (rows, bases), 1)
    ).astype(jnp.bfloat16)
    keep = (
        lax.broadcasted_iota(jnp.int32, (rows, columns), 0) // bases
        == lax.broadcasted_iota(jnp.int32, (rows, columns), 1) % GROUP
    )
    parts = []
    for half in halves(scale * mixing):
        wide = dot(half, pick, ((0,), (0,))).astype(jnp.bfloat16)
        parts.append(jnp.where(keep, dot(tile, wide), 0.0).astype(jnp.bfloat16))
    return jnp.concatenate(parts, axis=1)


def call(kernel, out_shape, *args, grid=(), in_specs=None, out_specs=None, scratch=(), flops=0, traffic=0, limit=40):
    whole = pl.BlockSpec(memory_space=pltpu.VMEM)
    single = isinstance(out_shape, jax.ShapeDtypeStruct)
    return pl.pallas_call(
        kernel,
        out_shape=out_shape,
        grid=grid,
        in_specs=[whole] * len(args) if in_specs is None else in_specs,
        out_specs=(whole if single else [whole] * len(out_shape)) if out_specs is None else out_specs,
        scratch_shapes=list(scratch),
        compiler_params=pltpu.CompilerParams(vmem_limit_bytes=limit * MEGABYTE),
        cost_estimate=pl.CostEstimate(flops=flops, bytes_accessed=traffic, transcendentals=0),
    )(*args)


def shape_of(shape, dtype):
    return jax.ShapeDtypeStruct(tuple(shape), dtype)


def store_products(weights_ref, low, product_ref, gram_ref):
    product_ref[...] = dot(low, weights_ref[...], ((0,), (0,))).T
    gram_ref[...] = dot(low, low, ((0,), (0,)))


def start_kernel(row_ref, weights_ref, own_ref, other_ref, full_ref, low_ref, product_ref, gram_ref):
    rows = own_ref.shape[0]
    row = row_ref[0]
    full_ref[pl.ds(pl.multiple_of(row * rows, rows), rows), :] = own_ref[...]
    full_ref[pl.ds(pl.multiple_of((1 - row) * rows, rows), rows), :] = other_ref[...]
    low = full_ref[...].astype(jnp.bfloat16)
    low_ref[...] = low
    store_products(weights_ref, low, product_ref, gram_ref)


def step_kernel(weights_ref, full_ref, mine_ref, other_ref, low_ref, product_ref, gram_ref):
    gradient = mine_ref[...].astype(jnp.float32) + other_ref[...].astype(jnp.float32)
    low = first_step(full_ref[...], gradient, EPSILON_FACTORS).astype(jnp.bfloat16)
    low_ref[...] = low
    store_products(weights_ref, low, product_ref, gram_ref)


def panel_kernel(panels_ref, product_ref, gram_ref, out_ref):
    high, low = halves(gram_ref[...])
    panels = panels_ref[...]
    out_ref[...] = (dot(panels, high) + dot(panels, low) - product_ref[...]).astype(jnp.bfloat16)


def factor_kernel(weights_ref, low_ref, panels_ref, out_ref):
    panels = panels_ref[...]
    high, low = halves(dot(panels, panels, ((0,), (0,))))
    factors = low_ref[...]
    out_ref[...] = (
        dot(factors, high) + dot(factors, low) - dot(weights_ref[...], panels)
    ).astype(jnp.bfloat16)


def last_factor_kernel(row_ref, own_ref, mine_old_ref, other_old_ref, mine_ref, other_ref, out_ref):
    rows = own_ref.shape[0]
    here = pl.ds(pl.multiple_of(row_ref[0] * rows, rows), rows)
    old = mine_old_ref[here, :].astype(jnp.float32) + other_old_ref[here, :].astype(jnp.float32)
    new = mine_ref[here, :].astype(jnp.float32) + other_ref[here, :].astype(jnp.float32)
    out_ref[...] = second_step(own_ref[...], old, new, EPSILON_FACTORS)


def group_of(ref, position):
    block = ref[position * GROUP : (position + 1) * GROUP]
    return block.reshape(-1, block.shape[-1])


def blocks_of(ref, position):
    block = ref[:, position * GROUP : (position + 1) * GROUP, :]
    return block.reshape(-1, block.shape[-1])


def mix_groups(spread, bases_ref, out_ref):
    half = spread.shape[0] // 2
    for position in range(bases_ref.shape[0] // GROUP):
        both = dot(spread, group_of(bases_ref, position).astype(jnp.bfloat16))
        mixed = (both[:half] + both[half:]).astype(jnp.bfloat16)
        out_ref[:, position * GROUP : (position + 1) * GROUP, :] = mixed.reshape(-1, GROUP, mixed.shape[-1])


def mix_kernel(scale, mixing_ref, bases_ref, out_ref, spread):
    @pl.when(pl.program_id(0) == 0)
    def _():
        spread[...] = spread_rows(mixing_ref[...], scale)

    mix_groups(spread[...], bases_ref, out_ref)


def next_mix_kernel(scale, sums_ref, mixing_ref, bases_ref, out_ref, next_ref, grad_ref, spread):
    @pl.when(pl.program_id(0) == 0)
    def _():
        gradient = jnp.sum(sums_ref[...], axis=0)
        following = first_step(mixing_ref[...], gradient, EPSILON_MIXING)
        next_ref[...] = following
        grad_ref[...] = gradient
        spread[...] = spread_rows(following, scale)

    mix_groups(spread[...], bases_ref, out_ref)


def mixing_kernel(scale, bases_ref, blocks_ref, out_ref, total):
    step = pl.program_id(0)

    @pl.when(step == 0)
    def _():
        total[...] = jnp.zeros_like(total)

    count = bases_ref.shape[0] // GROUP
    left = jnp.concatenate([blocks_of(blocks_ref, position) for position in range(count)], axis=1)
    right = jnp.concatenate(
        [group_of(bases_ref, position).astype(jnp.bfloat16) for position in range(count)], axis=1
    )
    total[...] += dot(left, right, ((1,), (1,)))

    @pl.when(step == pl.num_programs(0) - 1)
    def _():
        rows, columns = total.shape
        experts, bases = rows // GROUP, columns // GROUP
        keep = (
            lax.broadcasted_iota(jnp.int32, (rows, columns), 0) % GROUP
            == lax.broadcasted_iota(jnp.int32, (rows, columns), 1) // bases
        )
        wide = jnp.where(keep, total[...], 0.0).reshape(experts, GROUP, columns).sum(axis=1)
        fold = (
            lax.broadcasted_iota(jnp.int32, (columns, bases), 0) % bases
            == lax.broadcasted_iota(jnp.int32, (columns, bases), 1)
        ).astype(jnp.float32)
        gradient = scale * lax.dot_general(
            wide, fold, (((1,), (0,)), ((), ())),
            precision=lax.Precision.HIGHEST, preferred_element_type=jnp.float32,
        )
        out_ref[...] = jnp.broadcast_to(gradient[None], out_ref.shape)


def gradient_group(spread, blocks_ref, position):
    blocks = blocks_of(blocks_ref, position)
    return dot(spread, jnp.concatenate([blocks, blocks], axis=0))


def base_kernel(scale, mixing_ref, bases_ref, blocks_ref, out_ref, spread):
    @pl.when(pl.program_id(0) == 0)
    def _():
        spread[...] = spread_columns(mixing_ref[...], scale)

    for position in range(bases_ref.shape[0] // GROUP):
        gradient = gradient_group(spread[...], blocks_ref, position)
        values = first_step(group_of(bases_ref, position), gradient, EPSILON_BASES)
        out_ref[position * GROUP : (position + 1) * GROUP] = values.astype(out_ref.dtype).reshape(
            GROUP, -1, values.shape[-1]
        )


def last_base_kernel(
    scale, old_ref, new_ref, bases_ref, old_blocks_ref, blocks_ref, out_ref, old_spread, spread
):
    @pl.when(pl.program_id(0) == 0)
    def _():
        old_spread[...] = spread_columns(old_ref[...], scale)
        spread[...] = spread_columns(new_ref[...], scale)

    for position in range(bases_ref.shape[0] // GROUP):
        old = gradient_group(old_spread[...], old_blocks_ref, position)
        new = gradient_group(spread[...], blocks_ref, position)
        values = second_step(group_of(bases_ref, position), old, new, EPSILON_BASES)
        out_ref[position * GROUP : (position + 1) * GROUP] = values.reshape(GROUP, -1, values.shape[-1])


def swap_rows(array):
    return lax.ppermute(array, "row", [(0, 1), (1, 0)])


def exchange(array):
    return lax.all_to_all(array, "expert", split_axis=0, concat_axis=0, tiled=True)


def kernel_body(weights, factors, mixing, shared_bases):
    bf16, f32 = jnp.bfloat16, jnp.float32
    weights = weights[0]
    factors = factors[0]
    height, width = weights.shape
    own_rows, rank = factors.shape
    columns, bases, _ = shared_bases.shape
    experts = width // columns
    devices = experts * (height // own_rows)
    scale = 1.0 / math.sqrt(bases * rank)
    row = lax.axis_index("row").reshape(1)
    expert = lax.axis_index("expert")
    scalar = pl.BlockSpec(memory_space=pltpu.SMEM)
    whole = pl.BlockSpec(memory_space=pltpu.VMEM)

    wide_flops = 2 * height * width * rank
    mix_flops = 2 * columns * GROUP * experts * bases * rank
    block_bytes = 2 * width * rank
    base_bytes = 4 * shared_bases.size

    steps = columns // CHUNK
    bases_spec = pl.BlockSpec((CHUNK, bases, rank), lambda s: (s, 0, 0))
    blocks_spec = pl.BlockSpec((experts, CHUNK, rank), lambda s: (0, s, 0))

    def fixed(*shape):
        return pl.BlockSpec(shape, lambda s: (0,) * len(shape))

    blocks = shape_of((experts, columns, rank), bf16)
    panels_shape = shape_of((width, rank), bf16)
    small = shape_of((experts, bases), f32)
    rows_spread = pltpu.VMEM((2 * experts * GROUP, GROUP * bases), bf16)
    columns_spread = pltpu.VMEM((GROUP * bases, 2 * experts * GROUP), bf16)
    products = [shape_of((height, rank), bf16), shape_of((width, rank), f32), shape_of((rank, rank), f32)]

    def factor_part(low, panels):
        return call(
            factor_kernel, shape_of((height, rank), bf16), weights, low, panels,
            flops=wide_flops, traffic=weights.size * 2 + block_bytes,
        )

    def panel_part(panels, product, gram):
        return call(
            panel_kernel, panels_shape, panels, product, gram, flops=wide_flops // 8, traffic=4 * block_bytes
        ).reshape(blocks.shape)

    def mixing_part(values, collected):
        return call(
            functools.partial(mixing_kernel, scale),
            shape_of((devices, experts, bases), f32), values, collected,
            grid=(steps,), in_specs=[bases_spec, blocks_spec],
            out_specs=fixed(devices, experts, bases),
            scratch=[pltpu.VMEM((experts * GROUP, GROUP * bases), f32)],
            flops=mix_flops, traffic=values.size * values.dtype.itemsize,
        )

    other = swap_rows(factors)
    mixing_all = exchange(jnp.broadcast_to(mixing, (experts, bases)))
    full, low_one, product_one, gram_one = call(
        start_kernel, [shape_of((height, rank), f32)] + products, row, weights, factors, other,
        in_specs=[scalar, whole, whole, whole],
        flops=wide_flops, traffic=weights.size * 2 + 4 * block_bytes,
    )

    mixed_one = call(
        functools.partial(mix_kernel, scale), blocks, mixing_all, shared_bases,
        grid=(steps,), in_specs=[fixed(experts, bases), bases_spec], out_specs=blocks_spec,
        scratch=[rows_spread], flops=2 * mix_flops, traffic=base_bytes,
    )
    panels_one = exchange(mixed_one).reshape(width, rank)
    collected_one = exchange(panel_part(panels_one, product_one, gram_one))
    mine_one = factor_part(low_one, panels_one)
    other_one = swap_rows(mine_one)
    low_two, product_two, gram_two = call(
        step_kernel, products, weights, full, mine_one, other_one,
        flops=wide_flops, traffic=weights.size * 2 + 4 * block_bytes,
    )
    partial_one = mixing_part(shared_bases, collected_one)
    sums_one = lax.all_to_all(partial_one, ("expert", "row"), split_axis=0, concat_axis=0, tiled=True)
    bases_one = call(
        functools.partial(base_kernel, scale), shape_of(shared_bases.shape, bf16),
        mixing_all, shared_bases, collected_one,
        grid=(steps,), in_specs=[fixed(experts, bases), bases_spec, blocks_spec], out_specs=bases_spec,
        scratch=[columns_spread], flops=2 * mix_flops, traffic=2 * base_bytes,
    )

    mixed_two, mixing_one, grad_one = call(
        functools.partial(next_mix_kernel, scale), [blocks, small, small], sums_one, mixing_all, bases_one,
        grid=(steps,),
        in_specs=[fixed(devices, experts, bases), fixed(experts, bases), bases_spec],
        out_specs=[blocks_spec, fixed(experts, bases), fixed(experts, bases)],
        scratch=[rows_spread], flops=2 * mix_flops, traffic=base_bytes // 2,
    )
    panels_two = exchange(mixed_two).reshape(width, rank)
    collected_two = exchange(panel_part(panels_two, product_two, gram_two))
    mine_two = factor_part(low_two, panels_two)
    other_two = swap_rows(mine_two)
    factors_new = call(
        last_factor_kernel, shape_of((own_rows, rank), f32),
        row, factors, mine_one, other_one, mine_two, other_two,
        in_specs=[scalar] + [whole] * 5, traffic=12 * own_rows * rank,
    )
    partial_two = mixing_part(bases_one, collected_two)
    sums_two = lax.all_to_all(partial_two, ("expert", "row"), split_axis=0, concat_axis=0, tiled=True)
    bases_new = call(
        functools.partial(last_base_kernel, scale), shape_of(shared_bases.shape, f32),
        mixing_all, mixing_one, shared_bases, collected_one, collected_two,
        grid=(steps,),
        in_specs=[fixed(experts, bases)] * 2 + [bases_spec, blocks_spec, blocks_spec],
        out_specs=bases_spec,
        scratch=[columns_spread, columns_spread], flops=4 * mix_flops, traffic=2 * base_bytes,
    )
    grad_two = lax.dynamic_slice_in_dim(jnp.sum(sums_two, axis=0), expert, 1, 0)
    mixing_new = second_step(
        mixing, lax.dynamic_slice_in_dim(grad_one, expert, 1, 0), grad_two, EPSILON_MIXING
    )
    return (factors_new[None], bases_new, mixing_new)


def factor_gradient(residual_low, panels):
    grad_factor = jnp.einsum(
        "ehc,ecr->ehr", residual_low, panels, preferred_element_type=jnp.float32
    )
    return lax.psum_scatter(
        grad_factor.astype(jnp.bfloat16), "row", scatter_dimension=1, tiled=True
    ).astype(jnp.float32)


def plain_body(weights, factors, mixing, shared_bases):
    mix_scale = 1.0 / math.sqrt(shared_bases.shape[1] * shared_bases.shape[2])
    local_experts = mixing.shape[0]
    mixing_state = lax.all_gather(mixing, "expert", axis=0, tiled=True)
    factor_state = factors
    factor_one = jnp.zeros(factor_state.shape, jnp.float32)
    factor_two = jnp.zeros(factor_state.shape, jnp.float32)
    mixing_one = jnp.zeros(mixing_state.shape, jnp.float32)
    mixing_two = jnp.zeros(mixing_state.shape, jnp.float32)
    bases_state = shared_bases
    bases_one = jnp.zeros(shared_bases.shape, jnp.float32)
    bases_two = jnp.zeros(shared_bases.shape, jnp.float32)
    for iteration in range(1, ITERS + 1):
        mixing_all = mixing_state
        factor_low = lax.all_gather(factor_state.astype(jnp.bfloat16), "row", axis=1, tiled=True)
        mixed = (
            mix_scale
            * jnp.einsum("ej,cjr->ecr", mixing_all, bases_state, precision=lax.Precision.HIGHEST)
        ).astype(jnp.bfloat16)
        panels = lax.all_to_all(mixed, "expert", split_axis=0, concat_axis=1, tiled=True)
        residual = jnp.einsum(
            "ehr,ecr->ehc", factor_low, panels, preferred_element_type=jnp.float32
        ) - weights.astype(jnp.float32)
        residual_low = residual.astype(jnp.bfloat16)
        grad_panel = jnp.einsum(
            "ehc,ehr->ecr", residual_low, factor_low, preferred_element_type=jnp.float32
        )
        collected = lax.all_to_all(
            grad_panel.astype(jnp.bfloat16), "expert", split_axis=1, concat_axis=0, tiled=True
        ).astype(grad_panel.dtype)
        grad_rows = factor_gradient(residual_low, panels)
        grad_bases = mix_scale * jnp.einsum(
            "ej,ecr->cjr", mixing_all, collected, precision=lax.Precision.HIGHEST
        )
        partial_mixing = mix_scale * jnp.einsum(
            "cjr,ecr->ej", bases_state, collected, precision=lax.Precision.HIGHEST
        )
        bases_state, bases_one, bases_two = adam_update(
            bases_state, bases_one, bases_two, grad_bases, iteration, EPSILON_BASES
        )
        grad_mixing = lax.psum(partial_mixing, ("expert", "row"))
        mixing_state, mixing_one, mixing_two = adam_update(
            mixing_state, mixing_one, mixing_two, grad_mixing, iteration, EPSILON_MIXING
        )
        factor_state, factor_one, factor_two = adam_update(
            factor_state, factor_one, factor_two, grad_rows, iteration, EPSILON_FACTORS
        )
    mixing_out = lax.dynamic_slice_in_dim(
        mixing_state, lax.axis_index("expert") * local_experts, local_experts, 0
    )
    return (factor_state, bases_state, mixing_out)


def body(weights, factors, mixing, shared_bases):
    columns, bases, rank = shared_bases.shape
    experts = weights.shape[2] // columns
    fits = (
        weights.shape[0] == 1
        and weights.shape[1] == 2 * factors.shape[1]
        and columns % CHUNK == 0
        and experts == 8
        and bases == 64
        and rank == 128
    )
    run = kernel_body if fits else plain_body
    return run(weights, factors, mixing, shared_bases)


def solution(mesh):
    placed = (
        P(("layer", "expert"), None, "row"),
        P(("layer", "expert"), "row", None),
        P(("layer", "expert"), None),
        P(("layer", "row", "expert"), None, None),
    )
    return jax.shard_map(
        body,
        mesh=mesh,
        in_specs=placed,
        out_specs=(
            P(("layer", "expert"), "row", None),
            P(("layer", "row", "expert"), None, None),
            P(("layer", "expert"), None),
        ),
        check_vma=False,
    )
```

```python
import functools
import math

import jax
import jax.numpy as jnp
from jax import lax
from jax.experimental import pallas as pl
from jax.experimental.pallas import tpu as pltpu
from jax.sharding import PartitionSpec as P

ITERS = 2


BETA_ONE = 0.9
BETA_TWO = 0.999
RATE = 0.3
EPSILON_FACTORS = 8.0
EPSILON_BASES = 6.0
EPSILON_MIXING = 300.0

FIRST_OLD = BETA_ONE * (1.0 - BETA_ONE) / (1.0 - BETA_ONE**2)
FIRST_NEW = (1.0 - BETA_ONE) / (1.0 - BETA_ONE**2)
SECOND_OLD = BETA_TWO * (1.0 - BETA_TWO) / (1.0 - BETA_TWO**2)
SECOND_NEW = (1.0 - BETA_TWO) / (1.0 - BETA_TWO**2)

GROUP = 16
CHUNK = 32
MEGABYTE = 1 << 20
TINY = 1e-30
TAIL = 16


def adam_update(values, moment_one, moment_two, gradient, iteration, epsilon):
    moment_one = BETA_ONE * moment_one + (1.0 - BETA_ONE) * gradient
    moment_two = BETA_TWO * moment_two + (1.0 - BETA_TWO) * gradient * gradient
    correct_one = 1.0 - BETA_ONE**iteration
    correct_two = 1.0 - BETA_TWO**iteration
    values = values - RATE * (moment_one / correct_one) / (
        jnp.sqrt(moment_two / correct_two) + epsilon
    )
    return (values, moment_one, moment_two)


def ratio(top, bottom):
    guess = pltpu.reciprocal(bottom, approx=True)
    return top * (guess * (2.0 - bottom * guess))


def first_step(values, gradient, epsilon):
    return values - ratio(RATE * gradient, jnp.abs(gradient) + epsilon)


def last_step(values, old, new, epsilon):
    top = (RATE * FIRST_OLD) * old + (RATE * FIRST_NEW) * new
    square = SECOND_OLD * (old * old) + SECOND_NEW * (new * new)
    return values - ratio(top, square * lax.rsqrt(square + TINY) + epsilon)


def second_step(values, old, new, epsilon):
    return last_step(first_step(values, old, epsilon), old, new, epsilon)


def halves(array):
    high = array.astype(jnp.bfloat16)
    low = (array - high.astype(jnp.float32)).astype(jnp.bfloat16)
    return (high, low)


def dot(left, right, contract=((1,), (0,))):
    return lax.dot_general(left, right, (contract, ((), ())), preferred_element_type=jnp.float32)


def spread_rows(mixing, scale):
    experts, bases = mixing.shape
    rows, columns = experts * GROUP, GROUP * bases
    pick = (
        (lax.broadcasted_iota(jnp.int32, (rows, experts), 0) >> 4)
        == lax.broadcasted_iota(jnp.int32, (rows, experts), 1)
    ).astype(jnp.bfloat16)
    tile = (
        lax.broadcasted_iota(jnp.int32, (bases, columns), 0)
        == (lax.broadcasted_iota(jnp.int32, (bases, columns), 1) & 63)
    ).astype(jnp.bfloat16)
    keep = (
        (lax.broadcasted_iota(jnp.int32, (rows, columns), 0) & 15)
        == (lax.broadcasted_iota(jnp.int32, (rows, columns), 1) >> 6)
    )
    parts = []
    for half in halves(scale * mixing):
        wide = dot(half, tile).astype(jnp.bfloat16)
        parts.append(jnp.where(keep, dot(pick, wide), 0.0).astype(jnp.bfloat16))
    return jnp.concatenate(parts, axis=0)


def spread_columns(mixing, scale):
    experts, bases = mixing.shape
    rows, columns = GROUP * bases, experts * GROUP
    pick = (
        lax.broadcasted_iota(jnp.int32, (experts, columns), 0)
        == (lax.broadcasted_iota(jnp.int32, (experts, columns), 1) >> 4)
    ).astype(jnp.bfloat16)
    tile = (
        (lax.broadcasted_iota(jnp.int32, (rows, bases), 0) & 63)
        == lax.broadcasted_iota(jnp.int32, (rows, bases), 1)
    ).astype(jnp.bfloat16)
    keep = (
        (lax.broadcasted_iota(jnp.int32, (rows, columns), 0) >> 6)
        == (lax.broadcasted_iota(jnp.int32, (rows, columns), 1) & 15)
    )
    parts = []
    for half in halves(scale * mixing):
        wide = dot(half, pick, ((0,), (0,))).astype(jnp.bfloat16)
        parts.append(jnp.where(keep, dot(tile, wide), 0.0).astype(jnp.bfloat16))
    return jnp.concatenate(parts, axis=1)


def far_memory(specs):
    return specs is not None and any(spec.memory_space == pltpu.HBM for spec in specs)


def call(kernel, out_shape, *args, grid=(), in_specs=None, out_specs=None, scratch=(), flops=0, traffic=0, limit=24):
    whole = pl.BlockSpec(memory_space=pltpu.VMEM)
    single = isinstance(out_shape, jax.ShapeDtypeStruct)
    return pl.pallas_call(
        kernel,
        out_shape=out_shape,
        grid=grid,
        in_specs=[whole] * len(args) if in_specs is None else in_specs,
        out_specs=(whole if single else [whole] * len(out_shape)) if out_specs is None else out_specs,
        scratch_shapes=list(scratch),
        compiler_params=pltpu.CompilerParams(vmem_limit_bytes=(61 if far_memory(in_specs) else limit) * MEGABYTE),
        cost_estimate=pl.CostEstimate(flops=flops, bytes_accessed=traffic, transcendentals=0),
    )(*args)


def shape_of(shape, dtype):
    return jax.ShapeDtypeStruct(tuple(shape), dtype)


def store_products(weights_ref, low, product_ref, gram_ref):
    product_ref[...] = dot(low, weights_ref[...], ((0,), (0,))).T
    gram_ref[...] = dot(low, low, ((0,), (0,)))


def start_kernel(
    row_ref, far_weights_ref, own_ref, other_ref, mixing_ref, full_ref, low_ref, out_ref, weights_ref, sem
):
    load = pltpu.make_async_copy(far_weights_ref, weights_ref, sem)
    load.start()
    rows = own_ref.shape[0]
    row = row_ref[0]
    full_ref[pl.ds(pl.multiple_of(row * rows, rows), rows), :] = own_ref[...]
    full_ref[pl.ds(pl.multiple_of((1 - row) * rows, rows), rows), :] = other_ref[...]
    low = full_ref[...].astype(jnp.bfloat16)
    low_ref[...] = low
    experts, height, rank = out_ref.shape
    columns = height - rank - TAIL
    gram = dot(low, low, ((0,), (0,)))
    high = gram.astype(jnp.bfloat16)
    out_ref[:, columns : columns + rank, :] = jnp.broadcast_to(high[None], (experts, rank, rank))
    diagonal = lax.broadcasted_iota(jnp.int32, gram.shape, 0) == lax.broadcasted_iota(jnp.int32, gram.shape, 1)
    rest = jnp.sum(jnp.where(diagonal, gram - high.astype(jnp.float32), 0.0), axis=0, keepdims=True)
    mixing = mixing_ref[...]
    mixing = jnp.concatenate([mixing, jnp.zeros((1, rank - mixing.shape[1]), jnp.float32)], axis=1)
    first = mixing.astype(jnp.bfloat16).astype(jnp.float32)
    second = (mixing - first).astype(jnp.bfloat16).astype(jnp.float32)
    third = mixing - first - second
    place = lax.broadcasted_iota(jnp.int32, (TAIL, rank), 0)
    tail = jnp.zeros((TAIL, rank), jnp.float32)
    for position, part in enumerate((first, second, third, rest)):
        tail = jnp.where(place == position, part, tail)
    out_ref[:, columns + rank :, :] = jnp.broadcast_to(tail.astype(jnp.bfloat16)[None], (experts, TAIL, rank))
    load.wait()
    product = dot(low, weights_ref[...], ((0,), (0,))).T.astype(jnp.bfloat16)
    out_ref[:, :columns, :] = product.reshape(experts, columns, rank)


def step_kernel(weights_ref, full_ref, mine_ref, other_ref, low_ref, product_ref, gram_ref):
    gradient = mine_ref[...] + other_ref[...]
    low = first_step(full_ref[...], gradient, EPSILON_FACTORS).astype(jnp.bfloat16)
    low_ref[...] = low
    store_products(weights_ref, low, product_ref, gram_ref)


def panel_kernel(panels_ref, product_ref, gram_ref, out_ref):
    high, low = halves(gram_ref[...])
    panels = panels_ref[...]
    out_ref[...] = (dot(panels, high) + dot(panels, low) - product_ref[...]).astype(jnp.bfloat16)


def factor_kernel(weights_ref, low_ref, panels_ref, out_ref):
    experts, _, rank = panels_ref.shape
    columns = weights_ref.shape[1] // experts
    panels = panels_ref[:, :columns, :].reshape(-1, rank)
    high, low = halves(dot(panels, panels, ((0,), (0,))))
    factors = low_ref[...]
    out_ref[...] = dot(factors, high) + dot(factors, low) - dot(weights_ref[...], panels)


def last_factor_kernel(row_ref, own_ref, mine_old_ref, other_old_ref, mine_ref, other_ref, out_ref):
    rows = own_ref.shape[0]
    here = pl.ds(pl.multiple_of(row_ref[0] * rows, rows), rows)
    old = mine_old_ref[here, :] + other_old_ref[here, :]
    new = mine_ref[here, :] + other_ref[here, :]
    out_ref[...] = second_step(own_ref[...], old, new, EPSILON_FACTORS)


def pair_of(ref, pair):
    start = pl.multiple_of(pair * 2 * GROUP, 2 * GROUP)
    parts = [ref[pl.ds(start + half * GROUP, GROUP)] for half in range(2)]
    return [part.reshape(-1, part.shape[-1]) for part in parts]


def blocks_of(ref, pair):
    start = pl.multiple_of(pair * 2 * GROUP, 2 * GROUP)
    parts = [ref[:, pl.ds(start + half * GROUP, GROUP), :] for half in range(2)]
    return jnp.concatenate([part.reshape(-1, part.shape[-1]) for part in parts], axis=1)


def put_pair(ref, pair, wide):
    rank = wide.shape[1] // 2
    start = pl.multiple_of(pair * 2 * GROUP, 2 * GROUP)
    for half in range(2):
        part = wide[:, half * rank : (half + 1) * rank].astype(ref.dtype)
        ref[pl.ds(start + half * GROUP, GROUP)] = part.reshape(GROUP, -1, rank)


def copy_of(source, target, sems, pair):
    part = pl.ds(pl.multiple_of(pair * CHUNK, CHUNK), CHUNK)
    return pltpu.make_async_copy(source.at[part], target.at[part], sems.at[pair])


def each_pair(columns, step):
    lax.fori_loop(0, columns // CHUNK, lambda pair, _: step(pair), None)


def start_copies(source, target, sems):
    each_pair(source.shape[0], lambda pair: copy_of(source, target, sems, pair).start())


def wait_copies(source, target, sems):
    each_pair(source.shape[0], lambda pair: copy_of(source, target, sems, pair).wait())


def run_pairs(source, target, sems, step, batch=3):
    count = source.shape[0] // CHUNK
    for first in range(0, count, batch):
        batch_pairs = range(first, min(first + batch, count))
        for pair in batch_pairs:
            copy_of(source, target, sems, pair).wait()
        for pair in batch_pairs:
            step(pair)


def low_pair(ref, pair):
    return jnp.concatenate([part.astype(jnp.bfloat16) for part in pair_of(ref, pair)], axis=1)


def low_rest_pair(ref, pair):
    parts = [halves(part) for part in pair_of(ref, pair)]
    return [jnp.concatenate(side, axis=1) for side in zip(*parts)]


def mix_groups(spread, bases_ref, bases, sems, out_ref):
    half = spread.shape[0] // 2
    rank = bases.shape[-1]

    def step(pair):
        if bases.dtype == jnp.float32:
            high, low = low_rest_pair(bases, pair)
            both = dot(spread[...], high)
            mixed = both[:half] + both[half:] + dot(spread[:half], low)
        else:
            both = dot(spread[...], low_pair(bases, pair))
            mixed = both[:half] + both[half:]
        mixed = mixed.astype(jnp.bfloat16)
        start = pair * CHUNK
        for part in range(2):
            out_ref[:, pl.ds(start + part * GROUP, GROUP), :] = mixed[:, part * rank : (part + 1) * rank].reshape(
                -1, GROUP, rank
            )

    run_pairs(bases_ref, bases, sems, step)


def fold_total(scale, total, lanes):
    rows, columns = total.shape
    experts = rows // GROUP
    keep = (lax.broadcasted_iota(jnp.int32, (rows, columns), 0) & 15) == (
        lax.broadcasted_iota(jnp.int32, (rows, columns), 1) >> 6
    )
    wide = jnp.where(keep, total[...], 0.0).reshape(experts, GROUP, columns).sum(axis=1)
    fold = (
        (lax.broadcasted_iota(jnp.int32, (columns, lanes), 0) & 63)
        == lax.broadcasted_iota(jnp.int32, (columns, lanes), 1)
    ).astype(jnp.float32)
    return scale * lax.dot_general(
        wide, fold, (((1,), (0,)), ((), ())),
        precision=lax.Precision.HIGHEST, preferred_element_type=jnp.float32,
    )


def first_kernel(scale, sent_ref, bases_ref, out_ref, blocks_ref, mixing_ref, spread, total, blocks_rest, bases, sems):
    start_copies(bases_ref, bases, sems)
    columns, count, rank = bases.shape
    experts = sent_ref.shape[0]
    tail = sent_ref[:, columns + rank :, :].astype(jnp.float32)
    place = lax.broadcasted_iota(jnp.int32, tail.shape, 1)
    mixing = jnp.sum(jnp.where(place < 3, tail, 0.0), axis=1)[:, :count]
    rest = jnp.sum(jnp.where(place == 3, tail, 0.0), axis=1)
    mixing_ref[...] = mixing
    spread[...] = spread_rows(mixing, scale)
    mix_groups(spread, bases_ref, bases, sems, out_ref)
    for expert in range(experts):
        mixed = out_ref[expert, :columns, :]
        blocks_ref[expert], blocks_rest[expert] = halves(
            dot(mixed, sent_ref[expert, columns : columns + rank, :])
            + mixed.astype(jnp.float32) * rest[expert : expert + 1]
            - sent_ref[expert, :columns, :].astype(jnp.float32)
        )
    half = total.shape[0]
    result = None
    for pair in range(columns // CHUNK):
        high, low = low_rest_pair(bases, pair)
        blocks = blocks_of(blocks_ref, pair)
        both = dot(jnp.concatenate([blocks, blocks_of(blocks_rest, pair)], axis=0), high, ((1,), (1,)))
        product = both[:half] + both[half:] + dot(blocks, low, ((1,), (1,)))
        result = product if result is None else result + product
    total[...] = result
    high, low = halves(fold_total(scale, total, rank))
    sums = jnp.concatenate([high, low], axis=0)
    out_ref[:, columns:, :] = jnp.broadcast_to(sums[None], (experts,) + sums.shape)


def sum_kernel(sent_ref, out_ref):
    experts, rank = out_ref.shape
    start = sent_ref.shape[1] - 2 * experts
    sums = jnp.sum(sent_ref[:, start:, :].astype(jnp.float32), axis=0)
    out_ref[...] = sums[:experts] + sums[experts:]


def next_mix_kernel(scale, mine_ref, other_ref, mixing_ref, bases_ref, out_ref, next_ref, grad_ref, spread, bases, sems):
    start_copies(bases_ref, bases, sems)
    mixing = mixing_ref[...]
    gradient = (mine_ref[...] + other_ref[...])[:, : mixing.shape[1]]
    following = first_step(mixing, gradient, EPSILON_MIXING)
    next_ref[...] = following
    grad_ref[...] = gradient
    spread[...] = spread_rows(following, scale)
    mix_groups(spread, bases_ref, bases, sems, out_ref)


def mixing_kernel(scale, bases_ref, blocks_ref, out_ref, total, bases, sems):
    start_copies(bases_ref, bases, sems)
    total[...] = jnp.zeros_like(total)

    def step(pair):
        total[...] += dot(blocks_of(blocks_ref, pair), low_pair(bases, pair), ((1,), (1,)))

    run_pairs(bases_ref, bases, sems, step)
    gradient = fold_total(scale, total, out_ref.shape[-1])
    out_ref[...] = jnp.broadcast_to(gradient[None], out_ref.shape)


def gradient_pair(spread, blocks_ref, pair):
    blocks = blocks_of(blocks_ref, pair)
    return dot(spread[...], jnp.concatenate([blocks, blocks], axis=0))


def base_kernel(scale, mixing_ref, bases_ref, blocks_ref, out_ref, spread, bases, result, sems, out_sems):
    start_copies(bases_ref, bases, sems)
    spread[...] = spread_columns(mixing_ref[...], scale)

    def step(pair):
        gradient = gradient_pair(spread, blocks_ref, pair)
        copy_of(bases_ref, bases, sems, pair).wait()
        values = jnp.concatenate(pair_of(bases, pair), axis=1)
        put_pair(result, pair, first_step(values, gradient, EPSILON_BASES))
        copy_of(result, out_ref, out_sems, pair).start()

    each_pair(bases.shape[0], step)
    wait_copies(result, out_ref, out_sems)


def last_base_kernel(
    scale, old_ref, new_ref, bases_ref, old_blocks_ref, blocks_ref, out_ref,
    old_spread, spread, bases, sems, out_sems,
):
    start_copies(bases_ref, bases, sems)
    old_scale, new_scale = math.sqrt(SECOND_OLD), math.sqrt(SECOND_NEW)
    old_spread[...] = spread_columns(old_ref[...], scale * old_scale)
    spread[...] = spread_columns(new_ref[...], scale * new_scale)

    def step(pair):
        old = gradient_pair(old_spread, old_blocks_ref, pair)
        new = gradient_pair(spread, blocks_ref, pair)
        copy_of(bases_ref, bases, sems, pair).wait()
        values = jnp.concatenate(pair_of(bases, pair), axis=1)
        top = (RATE * FIRST_OLD / old_scale) * old + (RATE * FIRST_NEW / new_scale) * new
        square = old * old + new * new
        put_pair(bases, pair, values - ratio(top, square * lax.rsqrt(square + TINY) + EPSILON_BASES))
        copy_of(bases, out_ref, out_sems, pair).start()

    each_pair(bases.shape[0], step)
    wait_copies(bases, out_ref, out_sems)


def last_mixing_kernel(expert_ref, mixing_ref, old_ref, sums_ref, out_ref):
    experts, bases = old_ref.shape
    mine = lax.broadcasted_iota(jnp.int32, (experts, bases), 0) == expert_ref[0]
    new = jnp.sum(sums_ref[...], axis=0)[:, :bases]
    old = jnp.sum(jnp.where(mine, old_ref[...], 0.0), axis=0, keepdims=True)
    new = jnp.sum(jnp.where(mine, new, 0.0), axis=0, keepdims=True)
    out_ref[...] = second_step(mixing_ref[...], old, new, EPSILON_MIXING)


def swap_rows(array):
    return lax.ppermute(array, "row", [(0, 1), (1, 0)])


def exchange(array):
    return lax.all_to_all(array, "expert", split_axis=0, concat_axis=0, tiled=True)


def kernel_body(weights, factors, mixing, shared_bases):
    bf16, f32 = jnp.bfloat16, jnp.float32
    weights = weights[0]
    factors = factors[0]
    height, width = weights.shape
    own_rows, rank = factors.shape
    columns, bases, _ = shared_bases.shape
    experts = width // columns
    devices = experts * (height // own_rows)
    scale = 1.0 / math.sqrt(bases * rank)
    row = lax.axis_index("row").reshape(1)
    expert = lax.axis_index("expert").reshape(1)
    scalar = pl.BlockSpec(memory_space=pltpu.SMEM)
    whole = pl.BlockSpec(memory_space=pltpu.VMEM)

    wide_flops = 2 * height * width * rank
    mix_flops = 2 * columns * GROUP * experts * bases * rank
    block_bytes = 2 * width * rank
    base_bytes = 4 * shared_bases.size

    far = pl.BlockSpec(memory_space=pltpu.HBM)
    sems = pltpu.SemaphoreType.DMA((columns // CHUNK,))
    wide_scratch = pltpu.VMEM(shared_bases.shape, f32)
    thin_scratch = pltpu.VMEM(shared_bases.shape, bf16)
    blocks = shape_of((experts, columns, rank), bf16)
    panels_shape = shape_of((width, rank), bf16)
    small = shape_of((experts, bases), f32)
    rows_spread = pltpu.VMEM((2 * experts * GROUP, GROUP * bases), bf16)
    columns_spread = pltpu.VMEM((GROUP * bases, 2 * experts * GROUP), bf16)
    products = [shape_of((height, rank), bf16), shape_of((width, rank), f32), shape_of((rank, rank), f32)]

    def factor_part(low, panels):
        return call(
            factor_kernel, shape_of((height, rank), f32), weights, low, panels,
            flops=wide_flops, traffic=weights.size * 2 + block_bytes,
        )

    def panel_part(panels, product, gram):
        return call(
            panel_kernel, panels_shape, panels, product, gram, flops=wide_flops // 8, traffic=4 * block_bytes
        ).reshape(blocks.shape)

    def mixing_part(values, collected):
        return call(
            functools.partial(mixing_kernel, scale),
            shape_of((devices, experts, rank), f32), values, collected,
            in_specs=[far, whole],
            scratch=[
                pltpu.VMEM((experts * GROUP, GROUP * bases), f32), pltpu.VMEM(values.shape, values.dtype), sems
            ],
            flops=mix_flops, traffic=values.size * values.dtype.itemsize,
        )

    full, low_one, sent = call(
        start_kernel,
        [shape_of((height, rank), f32), products[0], shape_of((experts, columns + rank + TAIL, rank), bf16)],
        row, weights, factors, swap_rows(factors), mixing,
        in_specs=[scalar, far] + [whole] * 3,
        scratch=[pltpu.VMEM(weights.shape, bf16), pltpu.SemaphoreType.DMA(())],
        flops=wide_flops, traffic=weights.size * 2 + 4 * block_bytes,
    )

    sent = exchange(sent)
    mixed_one, collected_one, mixing_all = call(
        functools.partial(first_kernel, scale),
        [shape_of((experts, columns + 2 * experts, rank), bf16), blocks, small], sent, shared_bases,
        in_specs=[whole, far],
        scratch=[
            rows_spread, pltpu.VMEM((experts * GROUP, GROUP * bases), f32), pltpu.VMEM(blocks.shape, bf16),
            wide_scratch, sems,
        ],
        flops=3 * mix_flops, traffic=base_bytes,
    )
    panels_one = exchange(mixed_one)
    def first_bases(dtype, coefficients):
        return call(
            functools.partial(base_kernel, scale), shape_of(shared_bases.shape, dtype),
            coefficients, shared_bases, collected_one,
            in_specs=[whole, far, whole], out_specs=far,
            scratch=[columns_spread, wide_scratch, pltpu.VMEM(shared_bases.shape, dtype), sems, sems],
            flops=2 * mix_flops, traffic=2 * base_bytes,
        )

    bases_one = first_bases(bf16, mixing_all)
    panels_one, bases_one = lax.optimization_barrier((panels_one, bases_one))
    sums_one = call(sum_kernel, shape_of((experts, rank), f32), panels_one)
    other_sums = swap_rows(sums_one)
    mine_one = factor_part(low_one, panels_one)
    other_one = swap_rows(mine_one)
    low_two, product_two, gram_two = call(
        step_kernel, products, weights, full, mine_one, other_one,
        flops=wide_flops, traffic=weights.size * 2 + 4 * block_bytes,
    )

    mixed_two, mixing_one, grad_one = call(
        functools.partial(next_mix_kernel, scale), [blocks, small, small], sums_one, other_sums, mixing_all, bases_one,
        in_specs=[whole, whole, whole, far], scratch=[rows_spread, thin_scratch, sems],
        flops=2 * mix_flops, traffic=base_bytes // 2,
    )
    panels_two = exchange(mixed_two)
    collected_two = exchange(panel_part(panels_two.reshape(width, rank), product_two, gram_two))
    mine_two = factor_part(low_two, panels_two)
    other_two = swap_rows(mine_two)
    factors_new = call(
        last_factor_kernel, shape_of((own_rows, rank), f32),
        row, factors, mine_one, other_one, mine_two, other_two,
        in_specs=[scalar] + [whole] * 5, traffic=12 * own_rows * rank,
    )
    partial_two = mixing_part(bases_one, collected_two)
    sums_two = lax.all_to_all(partial_two, ("expert", "row"), split_axis=0, concat_axis=0, tiled=True)
    bases_new = call(
        functools.partial(last_base_kernel, scale), shape_of(shared_bases.shape, f32),
        mixing_all, mixing_one, first_bases(f32, mixing_all), collected_one, collected_two,
        in_specs=[whole, whole, far, whole, whole], out_specs=far,
        scratch=[columns_spread, columns_spread, wide_scratch, sems, sems], flops=4 * mix_flops, traffic=2 * base_bytes,
    )
    mixing_new = call(
        last_mixing_kernel, shape_of(mixing.shape, f32), expert, mixing, grad_one, sums_two,
        in_specs=[scalar] + [whole] * 3,
    )
    return (factors_new[None], bases_new, mixing_new)


def factor_gradient(residual_low, panels):
    grad_factor = jnp.einsum(
        "ehc,ecr->ehr", residual_low, panels, preferred_element_type=jnp.float32
    )
    return lax.psum_scatter(
        grad_factor.astype(jnp.bfloat16), "row", scatter_dimension=1, tiled=True
    ).astype(jnp.float32)


def plain_body(weights, factors, mixing, shared_bases):
    mix_scale = 1.0 / math.sqrt(shared_bases.shape[1] * shared_bases.shape[2])
    local_experts = mixing.shape[0]
    mixing_state = lax.all_gather(mixing, "expert", axis=0, tiled=True)
    factor_state = factors
    factor_one = jnp.zeros(factor_state.shape, jnp.float32)
    factor_two = jnp.zeros(factor_state.shape, jnp.float32)
    mixing_one = jnp.zeros(mixing_state.shape, jnp.float32)
    mixing_two = jnp.zeros(mixing_state.shape, jnp.float32)
    bases_state = shared_bases
    bases_one = jnp.zeros(shared_bases.shape, jnp.float32)
    bases_two = jnp.zeros(shared_bases.shape, jnp.float32)
    for iteration in range(1, ITERS + 1):
        mixing_all = mixing_state
        factor_low = lax.all_gather(factor_state.astype(jnp.bfloat16), "row", axis=1, tiled=True)
        mixed = (
            mix_scale
            * jnp.einsum("ej,cjr->ecr", mixing_all, bases_state, precision=lax.Precision.HIGHEST)
        ).astype(jnp.bfloat16)
        panels = lax.all_to_all(mixed, "expert", split_axis=0, concat_axis=1, tiled=True)
        residual = jnp.einsum(
            "ehr,ecr->ehc", factor_low, panels, preferred_element_type=jnp.float32
        ) - weights.astype(jnp.float32)
        residual_low = residual.astype(jnp.bfloat16)
        grad_panel = jnp.einsum(
            "ehc,ehr->ecr", residual_low, factor_low, preferred_element_type=jnp.float32
        )
        collected = lax.all_to_all(
            grad_panel.astype(jnp.bfloat16), "expert", split_axis=1, concat_axis=0, tiled=True
        ).astype(grad_panel.dtype)
        grad_rows = factor_gradient(residual_low, panels)
        grad_bases = mix_scale * jnp.einsum(
            "ej,ecr->cjr", mixing_all, collected, precision=lax.Precision.HIGHEST
        )
        partial_mixing = mix_scale * jnp.einsum(
            "cjr,ecr->ej", bases_state, collected, precision=lax.Precision.HIGHEST
        )
        bases_state, bases_one, bases_two = adam_update(
            bases_state, bases_one, bases_two, grad_bases, iteration, EPSILON_BASES
        )
        grad_mixing = lax.psum(partial_mixing, ("expert", "row"))
        mixing_state, mixing_one, mixing_two = adam_update(
            mixing_state, mixing_one, mixing_two, grad_mixing, iteration, EPSILON_MIXING
        )
        factor_state, factor_one, factor_two = adam_update(
            factor_state, factor_one, factor_two, grad_rows, iteration, EPSILON_FACTORS
        )
    mixing_out = lax.dynamic_slice_in_dim(
        mixing_state, lax.axis_index("expert") * local_experts, local_experts, 0
    )
    return (factor_state, bases_state, mixing_out)


def body(weights, factors, mixing, shared_bases):
    columns, bases, rank = shared_bases.shape
    experts = weights.shape[2] // columns
    fits = (
        weights.shape[0] == 1
        and weights.shape[1] == 2 * factors.shape[1]
        and columns % CHUNK == 0
        and experts == 8
        and bases == 64
        and rank == 128
        and 2 * experts == TAIL
    )
    run = kernel_body if fits else plain_body
    return run(weights, factors, mixing, shared_bases)


def solution(mesh):
    placed = (
        P(("layer", "expert"), None, "row"),
        P(("layer", "expert"), "row", None),
        P(("layer", "expert"), None),
        P(("layer", "row", "expert"), None, None),
    )
    return jax.shard_map(
        body,
        mesh=mesh,
        in_specs=placed,
        out_specs=(
            P(("layer", "expert"), "row", None),
            P(("layer", "row", "expert"), None, None),
            P(("layer", "expert"), None),
        ),
        check_vma=False,
    )
```

```python
import functools
import math

import jax
import jax.numpy as jnp
from jax import lax
from jax.experimental import pallas as pl
from jax.experimental.pallas import tpu as pltpu
from jax.sharding import PartitionSpec as P

ITERS = 2


BETA_ONE = 0.9
BETA_TWO = 0.999
RATE = 0.3
EPSILON_FACTORS = 8.0
EPSILON_BASES = 6.0
EPSILON_MIXING = 300.0

FIRST_OLD = BETA_ONE * (1.0 - BETA_ONE) / (1.0 - BETA_ONE**2)
FIRST_NEW = (1.0 - BETA_ONE) / (1.0 - BETA_ONE**2)
SECOND_OLD = BETA_TWO * (1.0 - BETA_TWO) / (1.0 - BETA_TWO**2)
SECOND_NEW = (1.0 - BETA_TWO) / (1.0 - BETA_TWO**2)

GROUP = 16
CHUNK = 32
MEGABYTE = 1 << 20
TINY = 1e-30
TAIL = 16


def adam_update(values, moment_one, moment_two, gradient, iteration, epsilon):
    moment_one = BETA_ONE * moment_one + (1.0 - BETA_ONE) * gradient
    moment_two = BETA_TWO * moment_two + (1.0 - BETA_TWO) * gradient * gradient
    correct_one = 1.0 - BETA_ONE**iteration
    correct_two = 1.0 - BETA_TWO**iteration
    values = values - RATE * (moment_one / correct_one) / (
        jnp.sqrt(moment_two / correct_two) + epsilon
    )
    return (values, moment_one, moment_two)


def ratio(top, bottom):
    guess = pltpu.reciprocal(bottom, approx=True)
    return top * (guess * (2.0 - bottom * guess))


def first_step(values, gradient, epsilon):
    return values - ratio(RATE * gradient, jnp.abs(gradient) + epsilon)


def last_step(values, old, new, epsilon):
    top = (RATE * FIRST_OLD) * old + (RATE * FIRST_NEW) * new
    square = SECOND_OLD * (old * old) + SECOND_NEW * (new * new)
    return values - ratio(top, square * lax.rsqrt(square + TINY) + epsilon)


def second_step(values, old, new, epsilon):
    return last_step(first_step(values, old, epsilon), old, new, epsilon)


def halves(array):
    high = array.astype(jnp.bfloat16)
    low = (array - high.astype(jnp.float32)).astype(jnp.bfloat16)
    return (high, low)


def dot(left, right, contract=((1,), (0,))):
    return lax.dot_general(left, right, (contract, ((), ())), preferred_element_type=jnp.float32)


def spread_rows(mixing, scale):
    experts, bases = mixing.shape
    rows, columns = experts * GROUP, GROUP * bases
    pick = (
        (lax.broadcasted_iota(jnp.int32, (rows, experts), 0) >> 4)
        == lax.broadcasted_iota(jnp.int32, (rows, experts), 1)
    ).astype(jnp.bfloat16)
    tile = (
        lax.broadcasted_iota(jnp.int32, (bases, columns), 0)
        == (lax.broadcasted_iota(jnp.int32, (bases, columns), 1) & 63)
    ).astype(jnp.bfloat16)
    keep = (
        (lax.broadcasted_iota(jnp.int32, (rows, columns), 0) & 15)
        == (lax.broadcasted_iota(jnp.int32, (rows, columns), 1) >> 6)
    )
    parts = []
    for half in halves(scale * mixing):
        wide = dot(half, tile).astype(jnp.bfloat16)
        parts.append(jnp.where(keep, dot(pick, wide), 0.0).astype(jnp.bfloat16))
    return jnp.concatenate(parts, axis=0)


def spread_columns(mixing, scale):
    experts, bases = mixing.shape
    rows, columns = GROUP * bases, experts * GROUP
    pick = (
        lax.broadcasted_iota(jnp.int32, (experts, columns), 0)
        == (lax.broadcasted_iota(jnp.int32, (experts, columns), 1) >> 4)
    ).astype(jnp.bfloat16)
    tile = (
        (lax.broadcasted_iota(jnp.int32, (rows, bases), 0) & 63)
        == lax.broadcasted_iota(jnp.int32, (rows, bases), 1)
    ).astype(jnp.bfloat16)
    keep = (
        (lax.broadcasted_iota(jnp.int32, (rows, columns), 0) >> 6)
        == (lax.broadcasted_iota(jnp.int32, (rows, columns), 1) & 15)
    )
    parts = []
    for half in halves(scale * mixing):
        wide = dot(half, pick, ((0,), (0,))).astype(jnp.bfloat16)
        parts.append(jnp.where(keep, dot(tile, wide), 0.0).astype(jnp.bfloat16))
    return jnp.concatenate(parts, axis=1)


def far_memory(specs):
    return specs is not None and any(spec.memory_space == pltpu.HBM for spec in specs)


def call(kernel, out_shape, *args, grid=(), in_specs=None, out_specs=None, scratch=(), flops=0, traffic=0, limit=20):
    whole = pl.BlockSpec(memory_space=pltpu.VMEM)
    single = isinstance(out_shape, jax.ShapeDtypeStruct)
    return pl.pallas_call(
        kernel,
        out_shape=out_shape,
        grid=grid,
        in_specs=[whole] * len(args) if in_specs is None else in_specs,
        out_specs=(whole if single else [whole] * len(out_shape)) if out_specs is None else out_specs,
        scratch_shapes=list(scratch),
        compiler_params=pltpu.CompilerParams(vmem_limit_bytes=(61 if far_memory(in_specs) else limit) * MEGABYTE),
        cost_estimate=pl.CostEstimate(flops=flops, bytes_accessed=traffic, transcendentals=0),
    )(*args)


def shape_of(shape, dtype):
    return jax.ShapeDtypeStruct(tuple(shape), dtype)


def store_products(weights_ref, low, product_ref, gram_ref):
    product_ref[...] = dot(low, weights_ref[...], ((0,), (0,))).T
    gram_ref[...] = dot(low, low, ((0,), (0,)))


def start_kernel(
    weights_ref, full_ref, mixing_ref, low_ref, out_ref
):
    low = full_ref[...].astype(jnp.bfloat16)
    low_ref[...] = low
    experts, height, rank = out_ref.shape
    half = rank // 2
    end = height - TAIL
    columns = end - rank - half
    gram = dot(low, low, ((0,), (0,)))
    packed = []
    for part in halves(gram):
        corner = jnp.concatenate([part[half : half + half // 2, half:], part[half + half // 2 :, half:]], axis=1)
        packed += [part[:half], corner]
    packed = jnp.concatenate(packed, axis=0)
    out_ref[:, columns:end, :] = jnp.broadcast_to(packed[None], (experts,) + packed.shape)
    mixing = mixing_ref[...]
    mixing = jnp.concatenate([mixing, jnp.zeros((1, rank - mixing.shape[1]), jnp.float32)], axis=1)
    first = mixing.astype(jnp.bfloat16).astype(jnp.float32)
    second = (mixing - first).astype(jnp.bfloat16).astype(jnp.float32)
    third = mixing - first - second
    place = lax.broadcasted_iota(jnp.int32, (TAIL, rank), 0)
    tail = jnp.zeros((TAIL, rank), jnp.float32)
    for position, part in enumerate((first, second, third)):
        tail = jnp.where(place == position, part, tail)
    out_ref[:, end:, :] = jnp.broadcast_to(tail.astype(jnp.bfloat16)[None], (experts, TAIL, rank))
    product = dot(low, weights_ref[...], ((0,), (0,))).T.astype(jnp.bfloat16)
    out_ref[:, :columns, :] = product.reshape(experts, columns, rank)


def step_kernel(weights_ref, full_ref, mine_ref, other_ref, low_ref, product_ref, gram_ref):
    gradient = mine_ref[...] + other_ref[...]
    low = first_step(full_ref[...], gradient, EPSILON_FACTORS).astype(jnp.bfloat16)
    low_ref[...] = low
    store_products(weights_ref, low, product_ref, gram_ref)


def panel_kernel(panels_ref, product_ref, gram_ref, out_ref):
    high, low = halves(gram_ref[...])
    panels = panels_ref[...]
    out_ref[...] = (dot(panels, high) + dot(panels, low) - product_ref[...]).astype(jnp.bfloat16)


def factor_kernel(weights_ref, low_ref, panels_ref, out_ref):
    experts, _, rank = panels_ref.shape
    columns = weights_ref.shape[1] // experts
    panels = panels_ref[:, :columns, :].reshape(-1, rank)
    high, low = halves(dot(panels, panels, ((0,), (0,))))
    factors = low_ref[...]
    out_ref[...] = dot(factors, high) + dot(factors, low) - dot(weights_ref[...], panels)


def last_factor_kernel(row_ref, own_ref, mine_old_ref, other_old_ref, mine_ref, other_ref, out_ref):
    rows = own_ref.shape[0]
    here = pl.ds(pl.multiple_of(row_ref[0] * rows, rows), rows)
    old = mine_old_ref[here, :] + other_old_ref[here, :]
    new = mine_ref[here, :] + other_ref[here, :]
    out_ref[...] = second_step(own_ref[...], old, new, EPSILON_FACTORS)


def pair_of(ref, pair):
    start = pl.multiple_of(pair * 2 * GROUP, 2 * GROUP)
    parts = [ref[pl.ds(start + half * GROUP, GROUP)] for half in range(2)]
    return [part.reshape(-1, part.shape[-1]) for part in parts]


def blocks_of(ref, pair):
    start = pl.multiple_of(pair * 2 * GROUP, 2 * GROUP)
    parts = [ref[:, pl.ds(start + half * GROUP, GROUP), :] for half in range(2)]
    return jnp.concatenate([part.reshape(-1, part.shape[-1]) for part in parts], axis=1)


def put_pair(ref, pair, wide):
    rank = wide.shape[1] // 2
    start = pl.multiple_of(pair * 2 * GROUP, 2 * GROUP)
    for half in range(2):
        part = wide[:, half * rank : (half + 1) * rank].astype(ref.dtype)
        ref[pl.ds(start + half * GROUP, GROUP)] = part.reshape(GROUP, -1, rank)


def copy_of(source, target, sems, pair):
    part = pl.ds(pl.multiple_of(pair * CHUNK, CHUNK), CHUNK)
    return pltpu.make_async_copy(source.at[part], target.at[part], sems.at[pair])


def each_pair(columns, step):
    lax.fori_loop(0, columns // CHUNK, lambda pair, _: step(pair), None)


def start_copies(source, target, sems):
    each_pair(source.shape[0], lambda pair: copy_of(source, target, sems, pair).start())


def wait_copies(source, target, sems):
    each_pair(source.shape[0], lambda pair: copy_of(source, target, sems, pair).wait())


def low_pair(ref, pair):
    return jnp.concatenate([part.astype(jnp.bfloat16) for part in pair_of(ref, pair)], axis=1)


def low_rest_pair(ref, pair):
    parts = [halves(part) for part in pair_of(ref, pair)]
    return [jnp.concatenate(side, axis=1) for side in zip(*parts)]


def put_mixed(out_ref, pair, wide):
    wide = wide.astype(jnp.bfloat16)
    rank = wide.shape[1] // 2
    start = pl.multiple_of(pair * CHUNK, CHUNK)
    for part in range(2):
        mixed = wide[:, part * rank : (part + 1) * rank]
        out_ref[:, pl.ds(start + part * GROUP, GROUP), :] = mixed.reshape(-1, GROUP, rank)


def fold_total(scale, total, lanes):
    rows, columns = total.shape
    experts = rows // GROUP
    keep = (lax.broadcasted_iota(jnp.int32, (rows, columns), 0) & 15) == (
        lax.broadcasted_iota(jnp.int32, (rows, columns), 1) >> 6
    )
    wide = jnp.where(keep, total[...], 0.0).reshape(experts, GROUP, columns).sum(axis=1)
    fold = (
        (lax.broadcasted_iota(jnp.int32, (columns, lanes), 0) & 63)
        == lax.broadcasted_iota(jnp.int32, (columns, lanes), 1)
    ).astype(jnp.float32)
    return scale * lax.dot_general(
        wide, fold, (((1,), (0,)), ((), ())),
        precision=lax.Precision.HIGHEST, preferred_element_type=jnp.float32,
    )


def first_kernel(
    scale, sent_ref, bases_ref, out_ref, blocks_ref, mixing_ref,
    spread, total, wide_blocks, grams, high_bases, low_bases, bases, sems,
):
    start_copies(bases_ref, bases, sems)
    columns, count, rank = bases.shape
    experts = sent_ref.shape[0]
    half = rank // 2
    for index in range(2 * experts):
        expert, start = index // 2, columns + (index % 2) * (half + half // 2)
        top = sent_ref[expert, start : start + half, :]
        packed = sent_ref[expert, start + half : start + half + half // 2, :]
        grams[index, :half, :] = top
        corner = jnp.concatenate([packed[:, :half], packed[:, half:]], axis=0)
        side = top[:, half:].astype(jnp.float32).T.astype(jnp.bfloat16)
        grams[index, half:, :] = jnp.concatenate([side, corner], axis=1)
    tail = sent_ref[:, columns + rank + half :, :].astype(jnp.float32)
    place = lax.broadcasted_iota(jnp.int32, tail.shape, 1)
    mixing = jnp.sum(jnp.where(place < 3, tail, 0.0), axis=1)[:, :count]
    mixing_ref[...] = mixing
    spread[...] = spread_rows(mixing, scale)
    half = spread.shape[0] // 2

    def mix(pair):
        copy_of(bases_ref, bases, sems, pair).wait()
        high, low = low_rest_pair(bases, pair)
        here = pl.ds(pl.multiple_of(pair * 2 * rank, 2 * rank), 2 * rank)
        high_bases[:, here] = high
        low_bases[:, here] = low
        both = dot(spread[...], high)
        put_mixed(out_ref, pair, both[:half] + both[half:] + dot(spread[:half], low))

    each_pair(columns, mix)
    for expert in range(experts):
        mixed = out_ref[expert, :columns, :]
        high, low = halves(
            dot(mixed, grams[2 * expert])
            + dot(mixed, grams[2 * expert + 1])
            - sent_ref[expert, :columns, :].astype(jnp.float32)
        )
        blocks_ref[expert] = high
        for position in range(columns // GROUP):
            rows = slice(position * GROUP, (position + 1) * GROUP)
            lanes = slice(position * rank, (position + 1) * rank)
            wide_blocks[expert * GROUP : (expert + 1) * GROUP, lanes] = high[rows]
            wide_blocks[half + expert * GROUP : half + (expert + 1) * GROUP, lanes] = low[rows]
    both = dot(wide_blocks[...], high_bases[...], ((1,), (1,)))
    total[...] = both[:half] + both[half:] + dot(wide_blocks[:half], low_bases[...], ((1,), (1,)))
    high, low = halves(fold_total(scale, total, rank))
    sums = jnp.concatenate([high, low], axis=0)
    out_ref[:, columns:, :] = jnp.broadcast_to(sums[None], (experts,) + sums.shape)


def sum_kernel(sent_ref, out_ref):
    experts, rank = out_ref.shape
    start = sent_ref.shape[1] - 2 * experts
    sums = jnp.sum(sent_ref[:, start:, :].astype(jnp.float32), axis=0)
    out_ref[...] = sums[:experts] + sums[experts:]


def next_mix_kernel(scale, mine_ref, other_ref, mixing_ref, bases_ref, out_ref, next_ref, grad_ref, spread):
    mixing = mixing_ref[...]
    gradient = (mine_ref[...] + other_ref[...])[:, : mixing.shape[1]]
    following = first_step(mixing, gradient, EPSILON_MIXING)
    next_ref[...] = following
    grad_ref[...] = gradient
    spread[...] = spread_rows(following, scale)
    half = spread.shape[0] // 2
    for pair in range(bases_ref.shape[0] // CHUNK):
        both = dot(spread[...], low_pair(bases_ref, pair))
        put_mixed(out_ref, pair, both[:half] + both[half:])


def mixing_kernel(scale, bases_ref, blocks_ref, out_ref, total):
    total[...] = sum(
        dot(blocks_of(blocks_ref, pair), low_pair(bases_ref, pair), ((1,), (1,)))
        for pair in range(bases_ref.shape[0] // CHUNK)
    )
    gradient = fold_total(scale, total, out_ref.shape[-1])
    out_ref[...] = jnp.broadcast_to(gradient[None], out_ref.shape)


def gradient_pair(spread, blocks_ref, pair):
    blocks = blocks_of(blocks_ref, pair)
    return dot(spread[...], jnp.concatenate([blocks, blocks], axis=0))


def base_kernel(scale, mixing_ref, bases_ref, blocks_ref, out_ref, spread, bases, result, sems, out_sems):
    start_copies(bases_ref, bases, sems)
    spread[...] = spread_columns(mixing_ref[...], scale)

    def step(pair):
        gradient = gradient_pair(spread, blocks_ref, pair)
        copy_of(bases_ref, bases, sems, pair).wait()
        values = jnp.concatenate(pair_of(bases, pair), axis=1)
        put_pair(result, pair, first_step(values, gradient, EPSILON_BASES))
        copy_of(result, out_ref, out_sems, pair).start()

    each_pair(bases.shape[0], step)
    wait_copies(result, out_ref, out_sems)


def last_base_kernel(
    scale, old_ref, new_ref, bases_ref, old_blocks_ref, blocks_ref, out_ref,
    old_spread, spread, bases, sems, out_sems,
):
    start_copies(bases_ref, bases, sems)
    old_scale, new_scale = math.sqrt(SECOND_OLD), math.sqrt(SECOND_NEW)
    old_spread[...] = spread_columns(old_ref[...], scale * old_scale)
    spread[...] = spread_columns(new_ref[...], scale * new_scale)

    def step(pair):
        old = gradient_pair(old_spread, old_blocks_ref, pair)
        new = gradient_pair(spread, blocks_ref, pair)
        copy_of(bases_ref, bases, sems, pair).wait()
        values = jnp.concatenate(pair_of(bases, pair), axis=1)
        top = (RATE * FIRST_OLD / old_scale) * old + (RATE * FIRST_NEW / new_scale) * new
        square = old * old + new * new
        put_pair(bases, pair, values - ratio(top, square * lax.rsqrt(square + TINY) + EPSILON_BASES))
        copy_of(bases, out_ref, out_sems, pair).start()

    each_pair(bases.shape[0], step)
    wait_copies(bases, out_ref, out_sems)


def last_mixing_kernel(expert_ref, mixing_ref, old_ref, sums_ref, out_ref):
    experts, bases = old_ref.shape
    mine = lax.broadcasted_iota(jnp.int32, (experts, bases), 0) == expert_ref[0]
    new = jnp.sum(sums_ref[...], axis=0)[:, :bases]
    old = jnp.sum(jnp.where(mine, old_ref[...], 0.0), axis=0, keepdims=True)
    new = jnp.sum(jnp.where(mine, new, 0.0), axis=0, keepdims=True)
    out_ref[...] = second_step(mixing_ref[...], old, new, EPSILON_MIXING)


def swap_rows(array):
    return lax.ppermute(array, "row", [(0, 1), (1, 0)])


def exchange(array):
    return lax.all_to_all(array, "expert", split_axis=0, concat_axis=0, tiled=True)


def kernel_body(weights, factors, mixing, shared_bases):
    bf16, f32 = jnp.bfloat16, jnp.float32
    weights = weights[0]
    factors = factors[0]
    height, width = weights.shape
    own_rows, rank = factors.shape
    columns, bases, _ = shared_bases.shape
    experts = width // columns
    devices = experts * (height // own_rows)
    scale = 1.0 / math.sqrt(bases * rank)
    row = lax.axis_index("row").reshape(1)
    expert = lax.axis_index("expert").reshape(1)
    scalar = pl.BlockSpec(memory_space=pltpu.SMEM)
    whole = pl.BlockSpec(memory_space=pltpu.VMEM)

    wide_flops = 2 * height * width * rank
    mix_flops = 2 * columns * GROUP * experts * bases * rank
    block_bytes = 2 * width * rank
    base_bytes = 4 * shared_bases.size

    far = pl.BlockSpec(memory_space=pltpu.HBM)
    sems = pltpu.SemaphoreType.DMA((columns // CHUNK,))
    wide_scratch = pltpu.VMEM(shared_bases.shape, f32)
    blocks = shape_of((experts, columns, rank), bf16)
    panels_shape = shape_of((width, rank), bf16)
    small = shape_of((experts, bases), f32)
    rows_spread = pltpu.VMEM((2 * experts * GROUP, GROUP * bases), bf16)
    columns_spread = pltpu.VMEM((GROUP * bases, 2 * experts * GROUP), bf16)
    products = [shape_of((height, rank), bf16), shape_of((width, rank), f32), shape_of((rank, rank), f32)]

    def factor_part(low, panels):
        return call(
            factor_kernel, shape_of((height, rank), f32), weights, low, panels,
            flops=wide_flops, traffic=weights.size * 2 + block_bytes,
        )

    def panel_part(panels, product, gram):
        return call(
            panel_kernel, panels_shape, panels, product, gram, flops=wide_flops // 8, traffic=4 * block_bytes
        ).reshape(blocks.shape)

    def mixing_part(values, collected):
        return call(
            functools.partial(mixing_kernel, scale),
            shape_of((devices, experts, rank), f32), values, collected,
            scratch=[pltpu.VMEM((experts * GROUP, GROUP * bases), f32)],
            flops=mix_flops, traffic=values.size * values.dtype.itemsize,
        )

    full = lax.all_gather(factors, "row", axis=0, tiled=True)
    low_one, sent = call(
        start_kernel,
        [products[0], shape_of((experts, columns + 3 * rank // 2 + TAIL, rank), bf16)],
        weights, full, mixing,
        flops=wide_flops, traffic=weights.size * 2 + 4 * block_bytes,
    )

    sent = exchange(sent)
    mixed_one, collected_one, mixing_all = call(
        functools.partial(first_kernel, scale),
        [shape_of((experts, columns + 2 * experts, rank), bf16), blocks, small], sent, shared_bases,
        in_specs=[whole, far],
        scratch=[
            rows_spread, pltpu.VMEM((experts * GROUP, GROUP * bases), f32),
            pltpu.VMEM((2 * experts * GROUP, columns // GROUP * rank), bf16),
            pltpu.VMEM((2 * experts, rank, rank), bf16), *[pltpu.VMEM((GROUP * bases, columns // GROUP * rank), bf16)] * 2,
            wide_scratch, sems,
        ],
        flops=3 * mix_flops, traffic=base_bytes,
    )
    panels_one = exchange(mixed_one)
    def first_bases(dtype, coefficients):
        return call(
            functools.partial(base_kernel, scale), shape_of(shared_bases.shape, dtype),
            coefficients, shared_bases, collected_one,
            in_specs=[whole, far, whole], out_specs=far,
            scratch=[columns_spread, wide_scratch, pltpu.VMEM(shared_bases.shape, dtype), sems, sems],
            flops=2 * mix_flops, traffic=2 * base_bytes,
        )

    bases_one = first_bases(bf16, mixing_all)
    panels_one, bases_one = lax.optimization_barrier((panels_one, bases_one))
    sums_one = call(sum_kernel, shape_of((experts, rank), f32), panels_one)
    other_sums = swap_rows(sums_one)
    mine_one = factor_part(low_one, panels_one)
    other_one = swap_rows(mine_one)
    low_two, product_two, gram_two = call(
        step_kernel, products, weights, full, mine_one, other_one,
        flops=wide_flops, traffic=weights.size * 2 + 4 * block_bytes,
    )

    mixed_two, mixing_one, grad_one = call(
        functools.partial(next_mix_kernel, scale), [blocks, small, small], sums_one, other_sums, mixing_all, bases_one,
        scratch=[rows_spread],
        flops=2 * mix_flops, traffic=base_bytes // 2,
    )
    panels_two = exchange(mixed_two)
    collected_two = exchange(panel_part(panels_two.reshape(width, rank), product_two, gram_two))
    mine_two = factor_part(low_two, panels_two)
    other_two = swap_rows(mine_two)
    factors_new = call(
        last_factor_kernel, shape_of((own_rows, rank), f32),
        row, factors, mine_one, other_one, mine_two, other_two,
        in_specs=[scalar] + [whole] * 5, traffic=12 * own_rows * rank,
    )
    partial_two = mixing_part(bases_one, collected_two)
    sums_two = lax.all_to_all(partial_two, ("expert", "row"), split_axis=0, concat_axis=0, tiled=True)
    bases_new = call(
        functools.partial(last_base_kernel, scale), shape_of(shared_bases.shape, f32),
        mixing_all, mixing_one, first_bases(f32, mixing_all), collected_one, collected_two,
        in_specs=[whole, whole, far, whole, whole], out_specs=far,
        scratch=[columns_spread, columns_spread, wide_scratch, sems, sems], flops=4 * mix_flops, traffic=2 * base_bytes,
    )
    mixing_new = call(
        last_mixing_kernel, shape_of(mixing.shape, f32), expert, mixing, grad_one, sums_two,
        in_specs=[scalar] + [whole] * 3,
    )
    return (factors_new[None], bases_new, mixing_new)


def factor_gradient(residual_low, panels):
    grad_factor = jnp.einsum(
        "ehc,ecr->ehr", residual_low, panels, preferred_element_type=jnp.float32
    )
    return lax.psum_scatter(
        grad_factor.astype(jnp.bfloat16), "row", scatter_dimension=1, tiled=True
    ).astype(jnp.float32)


def plain_body(weights, factors, mixing, shared_bases):
    mix_scale = 1.0 / math.sqrt(shared_bases.shape[1] * shared_bases.shape[2])
    local_experts = mixing.shape[0]
    mixing_state = lax.all_gather(mixing, "expert", axis=0, tiled=True)
    factor_state = factors
    factor_one = jnp.zeros(factor_state.shape, jnp.float32)
    factor_two = jnp.zeros(factor_state.shape, jnp.float32)
    mixing_one = jnp.zeros(mixing_state.shape, jnp.float32)
    mixing_two = jnp.zeros(mixing_state.shape, jnp.float32)
    bases_state = shared_bases
    bases_one = jnp.zeros(shared_bases.shape, jnp.float32)
    bases_two = jnp.zeros(shared_bases.shape, jnp.float32)
    for iteration in range(1, ITERS + 1):
        mixing_all = mixing_state
        factor_low = lax.all_gather(factor_state.astype(jnp.bfloat16), "row", axis=1, tiled=True)
        mixed = (
            mix_scale
            * jnp.einsum("ej,cjr->ecr", mixing_all, bases_state, precision=lax.Precision.HIGHEST)
        ).astype(jnp.bfloat16)
        panels = lax.all_to_all(mixed, "expert", split_axis=0, concat_axis=1, tiled=True)
        residual = jnp.einsum(
            "ehr,ecr->ehc", factor_low, panels, preferred_element_type=jnp.float32
        ) - weights.astype(jnp.float32)
        residual_low = residual.astype(jnp.bfloat16)
        grad_panel = jnp.einsum(
            "ehc,ehr->ecr", residual_low, factor_low, preferred_element_type=jnp.float32
        )
        collected = lax.all_to_all(
            grad_panel.astype(jnp.bfloat16), "expert", split_axis=1, concat_axis=0, tiled=True
        ).astype(grad_panel.dtype)
        grad_rows = factor_gradient(residual_low, panels)
        grad_bases = mix_scale * jnp.einsum(
            "ej,ecr->cjr", mixing_all, collected, precision=lax.Precision.HIGHEST
        )
        partial_mixing = mix_scale * jnp.einsum(
            "cjr,ecr->ej", bases_state, collected, precision=lax.Precision.HIGHEST
        )
        bases_state, bases_one, bases_two = adam_update(
            bases_state, bases_one, bases_two, grad_bases, iteration, EPSILON_BASES
        )
        grad_mixing = lax.psum(partial_mixing, ("expert", "row"))
        mixing_state, mixing_one, mixing_two = adam_update(
            mixing_state, mixing_one, mixing_two, grad_mixing, iteration, EPSILON_MIXING
        )
        factor_state, factor_one, factor_two = adam_update(
            factor_state, factor_one, factor_two, grad_rows, iteration, EPSILON_FACTORS
        )
    mixing_out = lax.dynamic_slice_in_dim(
        mixing_state, lax.axis_index("expert") * local_experts, local_experts, 0
    )
    return (factor_state, bases_state, mixing_out)


def body(weights, factors, mixing, shared_bases):
    columns, bases, rank = shared_bases.shape
    experts = weights.shape[2] // columns
    fits = (
        weights.shape[0] == 1
        and weights.shape[1] == 2 * factors.shape[1]
        and columns % CHUNK == 0
        and experts == 8
        and bases == 64
        and rank == 128
        and 2 * experts == TAIL
    )
    run = kernel_body if fits else plain_body
    return run(weights, factors, mixing, shared_bases)


def solution(mesh):
    placed = (
        P(("layer", "expert"), None, "row"),
        P(("layer", "expert"), "row", None),
        P(("layer", "expert"), None),
        P(("layer", "row", "expert"), None, None),
    )
    return jax.shard_map(
        body,
        mesh=mesh,
        in_specs=placed,
        out_specs=(
            P(("layer", "expert"), "row", None),
            P(("layer", "row", "expert"), None, None),
            P(("layer", "expert"), None),
        ),
        check_vma=False,
    )
```

```python
import functools
import math

import jax
import jax.numpy as jnp
from jax import lax
from jax.experimental import pallas as pl
from jax.experimental.pallas import tpu as pltpu
from jax.sharding import PartitionSpec as P

ITERS = 2


BETA_ONE = 0.9
BETA_TWO = 0.999
RATE = 0.3
EPSILON_FACTORS = 8.0
EPSILON_BASES = 6.0
EPSILON_MIXING = 300.0

FIRST_OLD = BETA_ONE * (1.0 - BETA_ONE) / (1.0 - BETA_ONE**2)
FIRST_NEW = (1.0 - BETA_ONE) / (1.0 - BETA_ONE**2)
SECOND_OLD = BETA_TWO * (1.0 - BETA_TWO) / (1.0 - BETA_TWO**2)
SECOND_NEW = (1.0 - BETA_TWO) / (1.0 - BETA_TWO**2)

GROUP = 16
CHUNK = 32
MEGABYTE = 1 << 20
TINY = 1e-30
TAIL = 16


def adam_update(values, moment_one, moment_two, gradient, iteration, epsilon):
    moment_one = BETA_ONE * moment_one + (1.0 - BETA_ONE) * gradient
    moment_two = BETA_TWO * moment_two + (1.0 - BETA_TWO) * gradient * gradient
    correct_one = 1.0 - BETA_ONE**iteration
    correct_two = 1.0 - BETA_TWO**iteration
    values = values - RATE * (moment_one / correct_one) / (
        jnp.sqrt(moment_two / correct_two) + epsilon
    )
    return (values, moment_one, moment_two)


def ratio(top, bottom):
    guess = pltpu.reciprocal(bottom, approx=True)
    return top * (guess * (2.0 - bottom * guess))


def first_step(values, gradient, epsilon):
    return values - ratio(RATE * gradient, jnp.abs(gradient) + epsilon)


def last_step(values, old, new, epsilon):
    top = (RATE * FIRST_OLD) * old + (RATE * FIRST_NEW) * new
    square = SECOND_OLD * (old * old) + SECOND_NEW * (new * new)
    return values - ratio(top, square * lax.rsqrt(square + TINY) + epsilon)


def second_step(values, old, new, epsilon):
    return last_step(first_step(values, old, epsilon), old, new, epsilon)


def halves(array):
    high = array.astype(jnp.bfloat16)
    low = (array - high.astype(jnp.float32)).astype(jnp.bfloat16)
    return (high, low)


def dot(left, right, contract=((1,), (0,))):
    return lax.dot_general(left, right, (contract, ((), ())), preferred_element_type=jnp.float32)


def spread_rows(mixing, scale):
    experts, bases = mixing.shape
    rows, columns = experts * GROUP, GROUP * bases
    pick = (
        (lax.broadcasted_iota(jnp.int32, (rows, experts), 0) >> 4)
        == lax.broadcasted_iota(jnp.int32, (rows, experts), 1)
    ).astype(jnp.bfloat16)
    tile = (
        lax.broadcasted_iota(jnp.int32, (bases, columns), 0)
        == (lax.broadcasted_iota(jnp.int32, (bases, columns), 1) & 63)
    ).astype(jnp.bfloat16)
    keep = (
        (lax.broadcasted_iota(jnp.int32, (rows, columns), 0) & 15)
        == (lax.broadcasted_iota(jnp.int32, (rows, columns), 1) >> 6)
    )
    parts = []
    for half in halves(scale * mixing):
        wide = dot(half, tile).astype(jnp.bfloat16)
        parts.append(jnp.where(keep, dot(pick, wide), 0.0).astype(jnp.bfloat16))
    return jnp.concatenate(parts, axis=0)


def spread_columns(mixing, scale):
    experts, bases = mixing.shape
    rows, columns = GROUP * bases, experts * GROUP
    pick = (
        lax.broadcasted_iota(jnp.int32, (experts, columns), 0)
        == (lax.broadcasted_iota(jnp.int32, (experts, columns), 1) >> 4)
    ).astype(jnp.bfloat16)
    tile = (
        (lax.broadcasted_iota(jnp.int32, (rows, bases), 0) & 63)
        == lax.broadcasted_iota(jnp.int32, (rows, bases), 1)
    ).astype(jnp.bfloat16)
    keep = (
        (lax.broadcasted_iota(jnp.int32, (rows, columns), 0) >> 6)
        == (lax.broadcasted_iota(jnp.int32, (rows, columns), 1) & 15)
    )
    parts = []
    for half in halves(scale * mixing):
        wide = dot(half, pick, ((0,), (0,))).astype(jnp.bfloat16)
        parts.append(jnp.where(keep, dot(tile, wide), 0.0).astype(jnp.bfloat16))
    return jnp.concatenate(parts, axis=1)


def far_memory(specs):
    return specs is not None and any(spec.memory_space == pltpu.HBM for spec in specs)


def call(kernel, out_shape, *args, grid=(), in_specs=None, out_specs=None, scratch=(), flops=0, traffic=0, limit=20):
    whole = pl.BlockSpec(memory_space=pltpu.VMEM)
    single = isinstance(out_shape, jax.ShapeDtypeStruct)
    return pl.pallas_call(
        kernel,
        out_shape=out_shape,
        grid=grid,
        in_specs=[whole] * len(args) if in_specs is None else in_specs,
        out_specs=(whole if single else [whole] * len(out_shape)) if out_specs is None else out_specs,
        scratch_shapes=list(scratch),
        compiler_params=pltpu.CompilerParams(vmem_limit_bytes=(61 if far_memory(in_specs) else limit) * MEGABYTE),
        cost_estimate=pl.CostEstimate(flops=flops, bytes_accessed=traffic, transcendentals=0),
    )(*args)


def shape_of(shape, dtype):
    return jax.ShapeDtypeStruct(tuple(shape), dtype)


def store_products(weights_ref, low, product_ref, gram_ref):
    product_ref[...] = dot(low, weights_ref[...], ((0,), (0,))).T
    gram_ref[...] = dot(low, low, ((0,), (0,)))


def start_kernel(
    weights_ref, full_ref, mixing_ref, low_ref, out_ref
):
    low = full_ref[...].astype(jnp.bfloat16)
    low_ref[...] = low
    experts, height, rank = out_ref.shape
    half = rank // 2
    end = height - TAIL
    columns = end - rank - half
    gram = dot(low, low, ((0,), (0,)))
    packed = []
    for part in halves(gram):
        corner = jnp.concatenate([part[half : half + half // 2, half:], part[half + half // 2 :, half:]], axis=1)
        packed += [part[:half], corner]
    packed = jnp.concatenate(packed, axis=0)
    out_ref[:, columns:end, :] = jnp.broadcast_to(packed[None], (experts,) + packed.shape)
    mixing = mixing_ref[...]
    mixing = jnp.concatenate([mixing, jnp.zeros((1, rank - mixing.shape[1]), jnp.float32)], axis=1)
    first = mixing.astype(jnp.bfloat16).astype(jnp.float32)
    second = (mixing - first).astype(jnp.bfloat16).astype(jnp.float32)
    third = mixing - first - second
    place = lax.broadcasted_iota(jnp.int32, (TAIL, rank), 0)
    tail = jnp.zeros((TAIL, rank), jnp.float32)
    for position, part in enumerate((first, second, third)):
        tail = jnp.where(place == position, part, tail)
    out_ref[:, end:, :] = jnp.broadcast_to(tail.astype(jnp.bfloat16)[None], (experts, TAIL, rank))
    product = dot(low, weights_ref[...], ((0,), (0,))).T.astype(jnp.bfloat16)
    out_ref[:, :columns, :] = product.reshape(experts, columns, rank)


def step_kernel(weights_ref, full_ref, mine_ref, other_ref, low_ref, product_ref, gram_ref):
    gradient = mine_ref[...] + other_ref[...]
    low = first_step(full_ref[...], gradient, EPSILON_FACTORS).astype(jnp.bfloat16)
    low_ref[...] = low
    store_products(weights_ref, low, product_ref, gram_ref)


def panel_kernel(panels_ref, product_ref, gram_ref, out_ref):
    high, low = halves(gram_ref[...])
    panels = panels_ref[...]
    out_ref[...] = (dot(panels, high) + dot(panels, low) - product_ref[...]).astype(jnp.bfloat16)


def factor_kernel(weights_ref, low_ref, panels_ref, out_ref):
    experts, _, rank = panels_ref.shape
    columns = weights_ref.shape[1] // experts
    panels = panels_ref[:, :columns, :].reshape(-1, rank)
    high, low = halves(dot(panels, panels, ((0,), (0,))))
    factors = low_ref[...]
    out_ref[...] = dot(factors, high) + dot(factors, low) - dot(weights_ref[...], panels)


def last_factor_kernel(row_ref, own_ref, mine_old_ref, other_old_ref, mine_ref, other_ref, out_ref):
    rows = own_ref.shape[0]
    here = pl.ds(pl.multiple_of(row_ref[0] * rows, rows), rows)
    old = mine_old_ref[here, :] + other_old_ref[here, :]
    new = mine_ref[here, :] + other_ref[here, :]
    out_ref[...] = second_step(own_ref[...], old, new, EPSILON_FACTORS)


def pair_of(ref, pair):
    start = pl.multiple_of(pair * 2 * GROUP, 2 * GROUP)
    parts = [ref[pl.ds(start + half * GROUP, GROUP)] for half in range(2)]
    return [part.reshape(-1, part.shape[-1]) for part in parts]


def blocks_of(ref, pair):
    start = pl.multiple_of(pair * 2 * GROUP, 2 * GROUP)
    parts = [ref[:, pl.ds(start + half * GROUP, GROUP), :] for half in range(2)]
    return jnp.concatenate([part.reshape(-1, part.shape[-1]) for part in parts], axis=1)


def put_pair(ref, pair, wide):
    rank = wide.shape[1] // 2
    start = pl.multiple_of(pair * 2 * GROUP, 2 * GROUP)
    for half in range(2):
        part = wide[:, half * rank : (half + 1) * rank].astype(ref.dtype)
        ref[pl.ds(start + half * GROUP, GROUP)] = part.reshape(GROUP, -1, rank)


def copy_of(source, target, sems, pair):
    part = pl.ds(pl.multiple_of(pair * CHUNK, CHUNK), CHUNK)
    return pltpu.make_async_copy(source.at[part], target.at[part], sems.at[pair])


def each_pair(columns, step):
    lax.fori_loop(0, columns // CHUNK, lambda pair, _: step(pair), None)


def start_copies(source, target, sems):
    each_pair(source.shape[0], lambda pair: copy_of(source, target, sems, pair).start())


def wait_copies(source, target, sems):
    each_pair(source.shape[0], lambda pair: copy_of(source, target, sems, pair).wait())


def low_pair(ref, pair):
    return jnp.concatenate([part.astype(jnp.bfloat16) for part in pair_of(ref, pair)], axis=1)


def low_rest_pair(ref, pair):
    parts = [halves(part) for part in pair_of(ref, pair)]
    return [jnp.concatenate(side, axis=1) for side in zip(*parts)]


def put_mixed(out_ref, pair, wide):
    wide = wide.astype(jnp.bfloat16)
    rank = wide.shape[1] // 2
    start = pl.multiple_of(pair * CHUNK, CHUNK)
    for part in range(2):
        mixed = wide[:, part * rank : (part + 1) * rank]
        out_ref[:, pl.ds(start + part * GROUP, GROUP), :] = mixed.reshape(-1, GROUP, rank)


def fold_total(scale, total, lanes):
    rows, columns = total.shape
    experts = rows // GROUP
    keep = (lax.broadcasted_iota(jnp.int32, (rows, columns), 0) & 15) == (
        lax.broadcasted_iota(jnp.int32, (rows, columns), 1) >> 6
    )
    wide = jnp.where(keep, total[...], 0.0).reshape(experts, GROUP, columns).sum(axis=1)
    fold = (
        (lax.broadcasted_iota(jnp.int32, (columns, lanes), 0) & 63)
        == lax.broadcasted_iota(jnp.int32, (columns, lanes), 1)
    ).astype(jnp.float32)
    return scale * lax.dot_general(
        wide, fold, (((1,), (0,)), ((), ())),
        precision=lax.Precision.HIGHEST, preferred_element_type=jnp.float32,
    )


def first_kernel(
    scale, sent_ref, bases_ref, out_ref, blocks_ref, mixing_ref,
    spread, total, wide_blocks, grams, high_bases, low_bases, bases, sems,
):
    start_copies(bases_ref, bases, sems)
    columns, count, rank = bases.shape
    experts = sent_ref.shape[0]
    half = rank // 2
    for index in range(2 * experts):
        expert, start = index // 2, columns + (index % 2) * (half + half // 2)
        top = sent_ref[expert, start : start + half, :]
        packed = sent_ref[expert, start + half : start + half + half // 2, :]
        grams[index, :half, :] = top
        corner = jnp.concatenate([packed[:, :half], packed[:, half:]], axis=0)
        side = top[:, half:].astype(jnp.float32).T.astype(jnp.bfloat16)
        grams[index, half:, :] = jnp.concatenate([side, corner], axis=1)
    tail = sent_ref[:, columns + rank + half :, :].astype(jnp.float32)
    place = lax.broadcasted_iota(jnp.int32, tail.shape, 1)
    mixing = jnp.sum(jnp.where(place < 3, tail, 0.0), axis=1)[:, :count]
    mixing_ref[...] = mixing
    spread[...] = spread_rows(mixing, scale)
    half = spread.shape[0] // 2

    def mix(pair):
        copy_of(bases_ref, bases, sems, pair).wait()
        high, low = low_rest_pair(bases, pair)
        here = pl.ds(pl.multiple_of(pair * 2 * rank, 2 * rank), 2 * rank)
        high_bases[:, here] = high
        low_bases[:, here] = low
        both = dot(spread[...], high)
        put_mixed(out_ref, pair, both[:half] + both[half:] + dot(spread[:half], low))

    each_pair(columns, mix)
    for expert in range(experts):
        mixed = out_ref[expert, :columns, :]
        high, low = halves(
            dot(mixed, grams[2 * expert])
            + dot(mixed, grams[2 * expert + 1])
            - sent_ref[expert, :columns, :].astype(jnp.float32)
        )
        blocks_ref[expert] = high
        for position in range(columns // GROUP):
            rows = slice(position * GROUP, (position + 1) * GROUP)
            lanes = slice(position * rank, (position + 1) * rank)
            wide_blocks[expert * GROUP : (expert + 1) * GROUP, lanes] = high[rows]
            wide_blocks[half + expert * GROUP : half + (expert + 1) * GROUP, lanes] = low[rows]
    both = dot(wide_blocks[...], high_bases[...], ((1,), (1,)))
    total[...] = both[:half] + both[half:] + dot(wide_blocks[:half], low_bases[...], ((1,), (1,)))
    high, low = halves(fold_total(scale, total, rank))
    sums = jnp.concatenate([high, low], axis=0)
    out_ref[:, columns:, :] = jnp.broadcast_to(sums[None], (experts,) + sums.shape)


def sum_kernel(sent_ref, out_ref):
    experts, rank = out_ref.shape
    start = sent_ref.shape[1] - 2 * experts
    sums = jnp.sum(sent_ref[:, start:, :].astype(jnp.float32), axis=0)
    out_ref[...] = sums[:experts] + sums[experts:]


def next_mix_kernel(scale, mine_ref, other_ref, mixing_ref, bases_ref, out_ref, next_ref, grad_ref, spread):
    mixing = mixing_ref[...]
    gradient = (mine_ref[...] + other_ref[...])[:, : mixing.shape[1]]
    following = first_step(mixing, gradient, EPSILON_MIXING)
    next_ref[...] = following
    grad_ref[...] = gradient
    spread[...] = spread_rows(following, scale)
    half = spread.shape[0] // 2
    for pair in range(bases_ref.shape[0] // CHUNK):
        both = dot(spread[...], low_pair(bases_ref, pair))
        put_mixed(out_ref, pair, both[:half] + both[half:])


def mixing_kernel(scale, bases_ref, blocks_ref, out_ref, total):
    total[...] = sum(
        dot(blocks_of(blocks_ref, pair), low_pair(bases_ref, pair), ((1,), (1,)))
        for pair in range(bases_ref.shape[0] // CHUNK)
    )
    gradient = fold_total(scale, total, out_ref.shape[-1])
    out_ref[...] = jnp.broadcast_to(gradient[None], out_ref.shape)


def gradient_pair(spread, blocks_ref, pair):
    blocks = blocks_of(blocks_ref, pair)
    return dot(spread[...], jnp.concatenate([blocks, blocks], axis=0))


def base_kernel(scale, mixing_ref, bases_ref, blocks_ref, out_ref, spread, bases, result, sems, out_sems):
    start_copies(bases_ref, bases, sems)
    spread[...] = spread_columns(mixing_ref[...], scale)

    def step(pair):
        gradient = gradient_pair(spread, blocks_ref, pair)
        copy_of(bases_ref, bases, sems, pair).wait()
        values = jnp.concatenate(pair_of(bases, pair), axis=1)
        put_pair(result, pair, first_step(values, gradient, EPSILON_BASES))
        copy_of(result, out_ref, out_sems, pair).start()

    each_pair(bases.shape[0], step)
    wait_copies(result, out_ref, out_sems)


def last_base_kernel(
    scale, old_ref, new_ref, bases_ref, old_blocks_ref, blocks_ref, out_ref,
    old_spread, spread, bases, sems, out_sems,
):
    start_copies(bases_ref, bases, sems)
    old_scale, new_scale = math.sqrt(SECOND_OLD), math.sqrt(SECOND_NEW)
    old_spread[...] = spread_columns(old_ref[...], scale * old_scale)
    spread[...] = spread_columns(new_ref[...], scale * new_scale)

    def step(pair):
        old = gradient_pair(old_spread, old_blocks_ref, pair)
        new = gradient_pair(spread, blocks_ref, pair)
        copy_of(bases_ref, bases, sems, pair).wait()
        values = jnp.concatenate(pair_of(bases, pair), axis=1)
        top = (RATE * FIRST_OLD / old_scale) * old + (RATE * FIRST_NEW / new_scale) * new
        square = old * old + new * new
        bottom = square * lax.rsqrt(square + TINY) + EPSILON_BASES
        put_pair(bases, pair, values - top * pltpu.reciprocal(bottom, approx=True))
        copy_of(bases, out_ref, out_sems, pair).start()

    each_pair(bases.shape[0], step)
    wait_copies(bases, out_ref, out_sems)


def last_mixing_kernel(expert_ref, mixing_ref, old_ref, sums_ref, out_ref):
    experts, bases = old_ref.shape
    mine = lax.broadcasted_iota(jnp.int32, (experts, bases), 0) == expert_ref[0]
    new = jnp.sum(sums_ref[...], axis=0)[:, :bases]
    old = jnp.sum(jnp.where(mine, old_ref[...], 0.0), axis=0, keepdims=True)
    new = jnp.sum(jnp.where(mine, new, 0.0), axis=0, keepdims=True)
    out_ref[...] = second_step(mixing_ref[...], old, new, EPSILON_MIXING)


def swap_rows(array):
    return lax.ppermute(array, "row", [(0, 1), (1, 0)])


def exchange(array):
    return lax.all_to_all(array, "expert", split_axis=0, concat_axis=0, tiled=True)


def kernel_body(weights, factors, mixing, shared_bases):
    bf16, f32 = jnp.bfloat16, jnp.float32
    weights = weights[0]
    factors = factors[0]
    height, width = weights.shape
    own_rows, rank = factors.shape
    columns, bases, _ = shared_bases.shape
    experts = width // columns
    devices = experts * (height // own_rows)
    scale = 1.0 / math.sqrt(bases * rank)
    row = lax.axis_index("row").reshape(1)
    expert = lax.axis_index("expert").reshape(1)
    scalar = pl.BlockSpec(memory_space=pltpu.SMEM)
    whole = pl.BlockSpec(memory_space=pltpu.VMEM)

    wide_flops = 2 * height * width * rank
    mix_flops = 2 * columns * GROUP * experts * bases * rank
    block_bytes = 2 * width * rank
    base_bytes = 4 * shared_bases.size

    far = pl.BlockSpec(memory_space=pltpu.HBM)
    sems = pltpu.SemaphoreType.DMA((columns // CHUNK,))
    wide_scratch = pltpu.VMEM(shared_bases.shape, f32)
    blocks = shape_of((experts, columns, rank), bf16)
    panels_shape = shape_of((width, rank), bf16)
    small = shape_of((experts, bases), f32)
    rows_spread = pltpu.VMEM((2 * experts * GROUP, GROUP * bases), bf16)
    columns_spread = pltpu.VMEM((GROUP * bases, 2 * experts * GROUP), bf16)
    products = [shape_of((height, rank), bf16), shape_of((width, rank), f32), shape_of((rank, rank), f32)]

    def factor_part(low, panels):
        return call(
            factor_kernel, shape_of((height, rank), f32), weights, low, panels,
            flops=wide_flops, traffic=weights.size * 2 + block_bytes,
        )

    def panel_part(panels, product, gram):
        return call(
            panel_kernel, panels_shape, panels, product, gram, flops=wide_flops // 8, traffic=4 * block_bytes
        ).reshape(blocks.shape)

    def mixing_part(values, collected):
        return call(
            functools.partial(mixing_kernel, scale),
            shape_of((devices, experts, rank), f32), values, collected,
            scratch=[pltpu.VMEM((experts * GROUP, GROUP * bases), f32)],
            flops=mix_flops, traffic=values.size * values.dtype.itemsize,
        )

    full = lax.all_gather(factors, "row", axis=0, tiled=True)
    low_one, sent = call(
        start_kernel,
        [products[0], shape_of((experts, columns + 3 * rank // 2 + TAIL, rank), bf16)],
        weights, full, mixing,
        flops=wide_flops, traffic=weights.size * 2 + 4 * block_bytes,
    )

    sent = exchange(sent)
    mixed_one, collected_one, mixing_all = call(
        functools.partial(first_kernel, scale),
        [shape_of((experts, columns + 2 * experts, rank), bf16), blocks, small], sent, shared_bases,
        in_specs=[whole, far],
        scratch=[
            rows_spread, pltpu.VMEM((experts * GROUP, GROUP * bases), f32),
            pltpu.VMEM((2 * experts * GROUP, columns // GROUP * rank), bf16),
            pltpu.VMEM((2 * experts, rank, rank), bf16), *[pltpu.VMEM((GROUP * bases, columns // GROUP * rank), bf16)] * 2,
            wide_scratch, sems,
        ],
        flops=3 * mix_flops, traffic=base_bytes,
    )
    panels_one = exchange(mixed_one)
    def first_bases(dtype, coefficients):
        return call(
            functools.partial(base_kernel, scale), shape_of(shared_bases.shape, dtype),
            coefficients, shared_bases, collected_one,
            in_specs=[whole, far, whole], out_specs=far,
            scratch=[columns_spread, wide_scratch, pltpu.VMEM(shared_bases.shape, dtype), sems, sems],
            flops=2 * mix_flops, traffic=2 * base_bytes,
        )

    bases_one = first_bases(bf16, mixing_all)
    panels_one, bases_one = lax.optimization_barrier((panels_one, bases_one))
    sums_one = call(sum_kernel, shape_of((experts, rank), f32), panels_one)
    other_sums = swap_rows(sums_one)
    mine_one = factor_part(low_one, panels_one)
    other_one = swap_rows(mine_one)
    low_two, product_two, gram_two = call(
        step_kernel, products, weights, full, mine_one, other_one,
        flops=wide_flops, traffic=weights.size * 2 + 4 * block_bytes,
    )

    mixed_two, mixing_one, grad_one = call(
        functools.partial(next_mix_kernel, scale), [blocks, small, small], sums_one, other_sums, mixing_all, bases_one,
        scratch=[rows_spread],
        flops=2 * mix_flops, traffic=base_bytes // 2,
    )
    panels_two = exchange(mixed_two)
    collected_two = exchange(panel_part(panels_two.reshape(width, rank), product_two, gram_two))
    mine_two = factor_part(low_two, panels_two)
    other_two = swap_rows(mine_two)
    factors_new = call(
        last_factor_kernel, shape_of((own_rows, rank), f32),
        row, factors, mine_one, other_one, mine_two, other_two,
        in_specs=[scalar] + [whole] * 5, traffic=12 * own_rows * rank,
    )
    partial_two = mixing_part(bases_one, collected_two)
    sums_two = lax.all_to_all(partial_two, ("expert", "row"), split_axis=0, concat_axis=0, tiled=True)
    bases_new = call(
        functools.partial(last_base_kernel, scale), shape_of(shared_bases.shape, f32),
        mixing_all, mixing_one, first_bases(f32, mixing_all), collected_one, collected_two,
        in_specs=[whole, whole, far, whole, whole], out_specs=far,
        scratch=[columns_spread, columns_spread, wide_scratch, sems, sems], flops=4 * mix_flops, traffic=2 * base_bytes,
    )
    mixing_new = call(
        last_mixing_kernel, shape_of(mixing.shape, f32), expert, mixing, grad_one, sums_two,
        in_specs=[scalar] + [whole] * 3,
    )
    return (factors_new[None], bases_new, mixing_new)


def factor_gradient(residual_low, panels):
    grad_factor = jnp.einsum(
        "ehc,ecr->ehr", residual_low, panels, preferred_element_type=jnp.float32
    )
    return lax.psum_scatter(
        grad_factor.astype(jnp.bfloat16), "row", scatter_dimension=1, tiled=True
    ).astype(jnp.float32)


def plain_body(weights, factors, mixing, shared_bases):
    mix_scale = 1.0 / math.sqrt(shared_bases.shape[1] * shared_bases.shape[2])
    local_experts = mixing.shape[0]
    mixing_state = lax.all_gather(mixing, "expert", axis=0, tiled=True)
    factor_state = factors
    factor_one = jnp.zeros(factor_state.shape, jnp.float32)
    factor_two = jnp.zeros(factor_state.shape, jnp.float32)
    mixing_one = jnp.zeros(mixing_state.shape, jnp.float32)
    mixing_two = jnp.zeros(mixing_state.shape, jnp.float32)
    bases_state = shared_bases
    bases_one = jnp.zeros(shared_bases.shape, jnp.float32)
    bases_two = jnp.zeros(shared_bases.shape, jnp.float32)
    for iteration in range(1, ITERS + 1):
        mixing_all = mixing_state
        factor_low = lax.all_gather(factor_state.astype(jnp.bfloat16), "row", axis=1, tiled=True)
        mixed = (
            mix_scale
            * jnp.einsum("ej,cjr->ecr", mixing_all, bases_state, precision=lax.Precision.HIGHEST)
        ).astype(jnp.bfloat16)
        panels = lax.all_to_all(mixed, "expert", split_axis=0, concat_axis=1, tiled=True)
        residual = jnp.einsum(
            "ehr,ecr->ehc", factor_low, panels, preferred_element_type=jnp.float32
        ) - weights.astype(jnp.float32)
        residual_low = residual.astype(jnp.bfloat16)
        grad_panel = jnp.einsum(
            "ehc,ehr->ecr", residual_low, factor_low, preferred_element_type=jnp.float32
        )
        collected = lax.all_to_all(
            grad_panel.astype(jnp.bfloat16), "expert", split_axis=1, concat_axis=0, tiled=True
        ).astype(grad_panel.dtype)
        grad_rows = factor_gradient(residual_low, panels)
        grad_bases = mix_scale * jnp.einsum(
            "ej,ecr->cjr", mixing_all, collected, precision=lax.Precision.HIGHEST
        )
        partial_mixing = mix_scale * jnp.einsum(
            "cjr,ecr->ej", bases_state, collected, precision=lax.Precision.HIGHEST
        )
        bases_state, bases_one, bases_two = adam_update(
            bases_state, bases_one, bases_two, grad_bases, iteration, EPSILON_BASES
        )
        grad_mixing = lax.psum(partial_mixing, ("expert", "row"))
        mixing_state, mixing_one, mixing_two = adam_update(
            mixing_state, mixing_one, mixing_two, grad_mixing, iteration, EPSILON_MIXING
        )
        factor_state, factor_one, factor_two = adam_update(
            factor_state, factor_one, factor_two, grad_rows, iteration, EPSILON_FACTORS
        )
    mixing_out = lax.dynamic_slice_in_dim(
        mixing_state, lax.axis_index("expert") * local_experts, local_experts, 0
    )
    return (factor_state, bases_state, mixing_out)


def body(weights, factors, mixing, shared_bases):
    columns, bases, rank = shared_bases.shape
    experts = weights.shape[2] // columns
    fits = (
        weights.shape[0] == 1
        and weights.shape[1] == 2 * factors.shape[1]
        and columns % CHUNK == 0
        and experts == 8
        and bases == 64
        and rank == 128
        and 2 * experts == TAIL
    )
    run = kernel_body if fits else plain_body
    return run(weights, factors, mixing, shared_bases)


def solution(mesh):
    placed = (
        P(("layer", "expert"), None, "row"),
        P(("layer", "expert"), "row", None),
        P(("layer", "expert"), None),
        P(("layer", "row", "expert"), None, None),
    )
    return jax.shard_map(
        body,
        mesh=mesh,
        in_specs=placed,
        out_specs=(
            P(("layer", "expert"), "row", None),
            P(("layer", "row", "expert"), None, None),
            P(("layer", "expert"), None),
        ),
        check_vma=False,
    )
```
